256 devices in a mesh: gx: 16 (over y_hi, x, core), gy: 16 (over z, y_lo).
Axes of the slice: x: 4, y: 4 (y_hi: 2, y_lo: 2; y = y_hi * 2 + y_lo), z: 8, core: 2. Of those that a mesh axis runs over, the one named last changes fastest.
Arguments:
- state: float32 [16, 16, 256, 8, 128], P('gx', 'gy'), may hold values from -4 to 6, as said below
- heavy_flag: int32 [16, 16], P('gx', 'gy'), may hold values from 0 to 1, as said below
- order: int32 [16, 16, 256], P('gx', 'gy'), may hold values from 0 to 255, as said below
- send: int32 [16, 16, 64], P('gx', 'gy'), may hold values from 0 to 255, as said below
- nbr: int32 [16, 16, 256, 8], P('gx', 'gy'), may hold values from -1 to 575, as said below
Outputs:
- rates: float32 [16, 16, 256, 4, 128], P('gx', 'gy')
The draws below stay inside these ranges and needn't reach their ends.
Inputs may be any that keep to these rules, and one draw needn't show every extreme that they name: `state`: components in order: position x, y, z in 0 to 6, velocity u, v, w in -4 to 4, density in 0.95 to 1.05, mass in 0.02 to 0.08. `heavy_flag`: the devices at gx index g and g + 8 of one gy column are a matched pair, and exactly one of the two has flag 1. `order`: A permutation of the device's 256 slots. On a light device the first 128 entries are its live tiles. `send`: distinct slots of the device; on a light device all among its live tiles. `nbr`: distinct entries per tile, each an index into the device's extended list or -1; the -1 entries stand at the end, at most 2 of them. No entry names a grid offset outside the grid, and none names a tile of the device itself that is not live.
All inputs are finite; a program needn't handle non-finite values.
Results may differ from the reference program's by a relative error of at most 0.0003.
Values sent between devices are 32-bit elements; how exact they have to be, the bound alone decides.
A program may use at most 64 MiB of HBM per device.

```python
import math
import jax
import jax.numpy as jnp
from jax import lax

TPD = 256
TILE = 128
NEIGHBOURS = 8
LIGHT = 128
HS_FACE = 64
HS_CORNER = 16
EXT = 576
N_GX = 16
N_GY = 16


OFFSETS = ((-1, -1), (-1, 0), (-1, 1), (0, -1), (0, 1), (1, -1), (1, 0), (1, 1))


BOX_SIDE = 6.0


def permute_slots(subkey, length):
    device_keys = jax.random.split(subkey, N_GX * N_GY)
    drawn = jax.vmap(lambda single: jax.random.permutation(single, length))(device_keys)
    return drawn.reshape(N_GX, N_GY, length).astype(jnp.int32)


def layout(key):
    base_key = jax.random.fold_in(key, 7)
    key_flip, key_order, key_heavy, key_light, key_score, key_pads = jax.random.split(base_key, 6)
    half_rows = N_GX // 2
    coin_flip = jax.random.randint(key_flip, (half_rows, N_GY), 0, 2).astype(jnp.int32)
    is_heavy = jnp.concatenate([coin_flip, 1 - coin_flip], axis=0)
    order = permute_slots(key_order, TPD)
    heavy_send = permute_slots(key_heavy, TPD)[:, :, :HS_FACE]
    light_pick = permute_slots(key_light, LIGHT)
    light_send = jnp.take_along_axis(order[:, :, :LIGHT], light_pick, axis=2)[:, :, :HS_FACE]
    send = jnp.where(is_heavy[:, :, None] == 1, heavy_send, light_send).astype(jnp.int32)
    slot_ids = jnp.arange(TPD, dtype=jnp.int32)
    member = jnp.any(order[:, :, :LIGHT, None] == slot_ids[None, None, None, :], axis=2)
    own_usable = (is_heavy[:, :, None] == 1) | member
    rows_at = jnp.arange(N_GX, dtype=jnp.int32)[:, None]
    cols_at = jnp.arange(N_GY, dtype=jnp.int32)[None, :]
    parts = [own_usable]
    for offset in OFFSETS:
        inside = (rows_at + offset[0] >= 0) & (rows_at + offset[0] < N_GX) & (cols_at + offset[1] >= 0) & (cols_at + offset[1] < N_GY)
        count = HS_CORNER if offset[0] != 0 and offset[1] != 0 else HS_FACE
        parts.append(jnp.repeat(inside[:, :, None], count, axis=2))
    usable = jnp.concatenate(parts, axis=2)
    scores = jax.random.randint(key_score, (N_GX, N_GY, TPD, EXT), 0, 2 ** 20)
    scores = jnp.where(usable[:, :, None, :], scores, 2 ** 30)
    chosen = jnp.argsort(scores, axis=3, stable=True)[..., :NEIGHBOURS].astype(jnp.int32)
    pad_count = jax.random.randint(key_pads, (N_GX, N_GY, TPD, 1), 0, NEIGHBOURS // 4 + 1)
    position = jnp.arange(NEIGHBOURS, dtype=jnp.int32)[None, None, None, :]
    nbr = jnp.where(position >= NEIGHBOURS - pad_count, -1, chosen).astype(jnp.int32)
    return (is_heavy, order, send, nbr)


def draw_heavy_flag(key, part):
    return layout(key)[0]


def draw_order(key, part):
    return layout(key)[1]


def draw_send(key, part):
    return layout(key)[2]


def draw_nbr(key, part):
    return layout(key)[3]


def draw_state(key, part):
    draw_keys = jax.random.split(jax.random.fold_in(key, 11), 4)
    leading = (N_GX, N_GY, TPD)
    position = jax.random.uniform(draw_keys[0], leading + (3, TILE), jnp.float32, 0.0, BOX_SIDE)
    velocity = jnp.clip(jax.random.normal(draw_keys[1], leading + (3, TILE), jnp.float32), -4.0, 4.0)
    density = jax.random.uniform(draw_keys[2], leading + (1, TILE), jnp.float32, 0.95, 1.05)
    log_mass = jax.random.uniform(draw_keys[3], leading + (1, TILE), jnp.float32, jnp.log(0.02), jnp.log(0.08))
    mass = jnp.clip(jnp.exp(log_mass), 0.02, 0.08)
    return jnp.concatenate([position, velocity, density, mass], axis=3).astype(jnp.float32)


def setup_inputs(seed: int = 0) -> dict:
    streams_of = jax.random.split(jax.random.key(seed), 6)
    return {
        "state": draw_state(jax.random.fold_in(streams_of[5], 71), 0),
        "heavy_flag": draw_heavy_flag(jax.random.fold_in(streams_of[5], 71), 0),
        "order": draw_order(jax.random.fold_in(streams_of[5], 71), 0),
        "send": draw_send(jax.random.fold_in(streams_of[5], 71), 0),
        "nbr": draw_nbr(jax.random.fold_in(streams_of[5], 71), 0),
    }


KERNEL_NORM = 21.0 / (16.0 * math.pi)
STIFFNESS = 5.0
SOUND_SPEED = math.sqrt(35.0)
VISCOSITY = 0.1
SOFTENING = 0.01

def pair_sums(own_tiles, other_tiles):
    sep_x = own_tiles[..., 0, :, None] - other_tiles[..., 0, None, :]
    sep_y = own_tiles[..., 1, :, None] - other_tiles[..., 1, None, :]
    sep_z = own_tiles[..., 2, :, None] - other_tiles[..., 2, None, :]
    rel_u = own_tiles[..., 3, :, None] - other_tiles[..., 3, None, :]
    rel_v = own_tiles[..., 4, :, None] - other_tiles[..., 4, None, :]
    rel_w = own_tiles[..., 5, :, None] - other_tiles[..., 5, None, :]
    rho_i = own_tiles[..., 6, :, None]
    rho_j = other_tiles[..., 6, None, :]
    mass_j = other_tiles[..., 7, None, :]
    dist_sq = sep_x * sep_x + sep_y * sep_y + sep_z * sep_z
    reach_left = jnp.maximum(1.0 - 0.5 * jnp.sqrt(dist_sq), 0.0)
    kernel_slope = -5.0 * KERNEL_NORM * reach_left * reach_left * reach_left
    press_i = STIFFNESS * (rho_i ** 7 - 1.0) / (rho_i * rho_i)
    press_j = STIFFNESS * (rho_j ** 7 - 1.0) / (rho_j * rho_j)
    closing = rel_u * sep_x + rel_v * sep_y + rel_w * sep_z
    viscous = -VISCOSITY * SOUND_SPEED * 2.0 * jnp.minimum(closing, 0.0) / ((dist_sq + SOFTENING) * (rho_i + rho_j))
    push_term = mass_j * (press_i + press_j + viscous) * kernel_slope
    accel_x = -lax.optimization_barrier(jnp.sum(push_term * sep_x, axis=-1))
    accel_y = -lax.optimization_barrier(jnp.sum(push_term * sep_y, axis=-1))
    accel_z = -lax.optimization_barrier(jnp.sum(push_term * sep_z, axis=-1))
    density_rate = lax.optimization_barrier(jnp.sum(mass_j * kernel_slope * closing, axis=-1))
    return jnp.stack([accel_x, accel_y, accel_z, density_rate], axis=-2)

def reference(state, heavy_flag, order, send, nbr):
    sent_tiles = jax.vmap(jax.vmap(lambda device_tiles, chosen_slots: device_tiles[chosen_slots]))(state, send)
    padded = jnp.pad(sent_tiles, ((1, 1), (1, 1), (0, 0), (0, 0), (0, 0)))
    blank_tile = jnp.zeros((8, TILE), jnp.float32).at[6].set(1.0)
    slot_ids = jnp.arange(TPD, dtype=jnp.int32)
    zero_index = jnp.zeros((), jnp.int32)

    def device_rates(device):
        row_index = (device // N_GY).astype(jnp.int32)
        col_index = (device % N_GY).astype(jnp.int32)
        own_tiles = state[row_index, col_index]
        halo_block = lax.dynamic_slice(padded, (row_index, col_index, zero_index, zero_index, zero_index), (3, 3, HS_FACE, 8, TILE))
        pieces = []
        for row_off in range(3):
            for col_off in range(3):
                if row_off == 1 and col_off == 1:
                    continue
                if row_off != 1 and col_off != 1:
                    pieces.append(halo_block[row_off, col_off, :HS_CORNER])
                else:
                    pieces.append(halo_block[row_off, col_off])
        extended = jnp.concatenate([own_tiles] + pieces + [blank_tile[None]], axis=0)
        tile_lists = nbr[row_index, col_index]
        tile_lists = jnp.where(tile_lists < 0, EXT, tile_lists).astype(jnp.int32)
        gathered = extended[tile_lists]
        tile_rates = lax.optimization_barrier(jnp.sum(pair_sums(own_tiles[:, None], gathered), axis=1))
        is_heavy = heavy_flag[row_index, col_index] == 1
        member = jnp.any(order[row_index, col_index, :LIGHT][:, None] == slot_ids[None, :], axis=0)
        live_mask = is_heavy | member
        return jnp.where(live_mask[:, None, None], tile_rates, 0.0)
    result = lax.map(device_rates, jnp.arange(N_GX * N_GY, dtype=jnp.int32))
    return result.reshape(N_GX, N_GY, TPD, 4, TILE)
```

```python
import math

import jax
import jax.numpy as jnp
from jax import lax
from jax.experimental import pallas as pl
from jax.experimental.pallas import tpu as pltpu
from jax.sharding import PartitionSpec as P

TPD = 256
NEIGHBOURS = 8
LIGHT = 128
HS_FACE = 64
HS_CORNER = 16
EXT = 576
OFFSETS = ((-1, -1), (-1, 0), (-1, 1), (0, -1), (0, 1), (1, -1), (1, 0), (1, 1))

SLOPE = -5.0 * 21.0 / (16.0 * math.pi)
ALPHA = 0.1 * math.sqrt(35.0) * 2.0
GAMMA = 2.0 / ALPHA
SOFT = 0.01 / 4.0
OWN_PART = (0, 0, 0, 1, 1, 2)
OTHER_PART = (0, 1, 2, 0, 1, 0)
BLOCKS = ((0, 0), (0, 1), (1, 0), (2, 0), (2, 1), (3, 0), (3, 1))
bf16, f32 = jnp.bfloat16, jnp.float32


def split3(v):
    hi = v.astype(bf16).astype(f32)
    rest = v - hi
    mid = rest.astype(bf16).astype(f32)
    return hi, mid, rest - mid


def fields(src, first):
    flat = src.reshape(src.shape[0] * 8, 128)

    def row(c):
        return flat[pl.ds(first * 8 + c, 8, stride=8), :]

    x, y, z = ((row(c) - 3.0) * 0.5 for c in range(3))
    u, v, w, rho, m = (row(c) for c in range(3, 8))
    r2 = rho * rho
    r4 = r2 * r2
    p = 5.0 * (r4 * r2 * rho - 1.0) / r2
    return x, y, z, u, v, w, rho, m, p, x * x + y * y + z * z, u * x + v * y + w * z


def other_rows(src, first):
    x, y, z, u, v, w, rho, m, p, xx, vx = fields(src, first)
    one = jnp.ones_like(x)
    gr = GAMMA * rho
    g2 = 2.0 * GAMMA
    return {
        (0, 3): 2.0 * x, (0, 4): 2.0 * y, (0, 5): 2.0 * z, (0, 7): xx, (0, 8): one,
        (1, 0): m * x, (1, 1): m * y, (1, 2): m * z, (1, 3): m * u, (1, 4): m * v, (1, 5): m * w,
        (1, 6): m, (1, 7): m * vx,
        (2, 3): 2.0 * gr * x, (2, 4): 2.0 * gr * y, (2, 5): 2.0 * gr * z, (2, 7): gr * (xx + SOFT), (2, 8): gr,
        (2, 9): g2 * x, (2, 10): g2 * y, (2, 11): g2 * z, (2, 12): GAMMA * one, (2, 13): GAMMA * xx,
        (3, 7): m * p, (3, 14): m,
    }


def own_rows(src, first):
    x, y, z, u, v, w, rho, m, p, xx, vx = fields(src, first)
    return (
        -u, -v, -w, -x, -y, -z, vx, jnp.ones_like(x),
        xx, -rho * x, -rho * y, -rho * z, rho * (xx + SOFT), rho, p,
    )


def other_tables(src, first, dest, stage, table, place):
    for (q, r), value in other_rows(src, first).items():
        b = BLOCKS.index((q, r // 8))
        for part, v in enumerate(split3(value)):
            stage[pl.ds(((b * 3 + part) * 8 + r % 8) * 8, 8), :] = v
    zero = jnp.zeros((8, 128), f32)
    for i in range(8):
        for part in range(3):
            for q in range(4):
                halves = [
                    stage[pl.ds((BLOCKS.index((q, h)) * 3 + part) * 64 + i, 8, stride=8), :]
                    if (q, h) in BLOCKS else zero
                    for h in range(2)
                ]
                at = part * 64 + q * 16
                table[dest + i, at:at + 16, :] = jnp.concatenate(halves, 0).astype(bf16)
        place[dest + i] = (src[first + i] - 3.0) * 0.5


def own_tables(src, first, stage, table):
    for r, value in enumerate(own_rows(src, first)):
        for part, v in enumerate(split3(value)):
            stage[pl.ds((((r // 8) * 3 + part) * 8 + r % 8) * 8, 8), :] = v
    for i in range(8):
        for part in range(3):
            for h in range(2):
                at = part * 16 + h * 8
                table[first + i, at:at + 8, :] = stage[pl.ds((h * 3 + part) * 64 + i, 8, stride=8), :]


def own_side(rows):
    parts = [rows[i * 16:(i + 1) * 16] for i in range(3)]
    return jnp.concatenate([parts[p] for p in OWN_PART], 0).T.astype(bf16)


def other_side(table, e):
    return jnp.concatenate(
        [
            jnp.concatenate([table[e, pl.ds(p * 64 + q * 16, 16), :] for p in OTHER_PART], 0)
            for q in range(4)
        ],
        1,
    )


def pair(own, other):
    g = jnp.dot(own, other, preferred_element_type=f32)
    h, c, d, a = (g[:, i * 128:(i + 1) * 128] for i in range(4))
    h = jnp.maximum(h, 1e-30)
    reach = jnp.maximum(1.0 - h * lax.rsqrt(h), 0.0)
    cube = reach * reach * reach
    push = (a - jnp.minimum(c, 0.0) * pl.reciprocal(d, approx=True)) * cube
    return push, cube * c


def tile_sums(own, entries, table, place):
    sums = None
    for e in entries:
        push, rate = pair(own, other_side(table, e))
        new = [push * place[e, 0:1], push * place[e, 1:2], push * place[e, 2:3], push, rate]
        sums = new if sums is None else [a + b for a, b in zip(sums, new)]
    return sums


def finish(acc, t, place, out):
    totals = [jnp.sum(acc[q].T, 0, keepdims=True) for q in range(5)]
    out[t, 0:3] = (-2.0 * SLOPE) * (place[t][:3] * totals[3] - jnp.concatenate(totals[:3], 0))
    out[t, 3:4] = (2.0 * SLOPE) * totals[4]


def rates_kernel(heavy, order, nbr, own, *rest):
    pieces, (out, stage, table, own_stage, own_table, acc, place, lists, counts) = rest[:8], rest[8:]
    stage[...] = jnp.zeros_like(stage)
    own_stage[...] = jnp.zeros_like(own_stage)
    live = LIGHT + (TPD - LIGHT) * heavy[0]

    base = 0
    for src in (own, *pieces):
        def build(b, _, src=src, base=base):
            other_tables(src, b * 8, base + b * 8, stage, table, place)
            return 0

        lax.fori_loop(0, src.shape[0] // 8, build, 0)
        base += src.shape[0]

    def build_own(b, _):
        own_tables(own, b * 8, own_stage, own_table)
        return 0

    lax.fori_loop(0, TPD // 8, build_own, 0)

    for g in range(3):
        counts[g] = 0

    def sort(s, _):
        t = order[s]
        g = jnp.where(nbr[t * NEIGHBOURS + 6] >= 0, 1, 0) + jnp.where(nbr[t * NEIGHBOURS + 7] >= 0, 1, 0)
        n = counts[g]
        lists[g * TPD + n] = t
        counts[g] = n + 1
        return 0

    lax.fori_loop(0, live, sort, 0)

    def clear(s, _):
        out[order[s]] = jnp.zeros((4, 128), f32)
        return 0

    lax.fori_loop(live, TPD, clear, 0)

    for g in range(3):
        n = counts[g]

        def tile(s, mine, g=g, n=n):
            t = lists[g * TPD + s]
            finish(acc, lists[g * TPD + jnp.maximum(s - 1, 0)], place, out)
            following = own_side(own_table[lists[g * TPD + jnp.minimum(s + 1, n - 1)]])
            entries = [nbr[t * NEIGHBOURS + k] for k in range(6 + g)]
            for q, value in enumerate(tile_sums(mine, entries, table, place)):
                acc[q] = value
            return following

        @pl.when(n > 0)
        def _(tile=tile, g=g, n=n):
            lax.fori_loop(0, n, tile, own_side(own_table[lists[g * TPD]]))
            finish(acc, lists[g * TPD + n - 1], place, out)


def shards(state, heavy_flag, order, send, nbr):
    own = state[0, 0]
    outgoing = jnp.take(own, send[0, 0], axis=0)
    n_gx, n_gy = lax.axis_size("gx"), lax.axis_size("gy")
    pieces = []
    for p, q in OFFSETS:
        count = HS_CORNER if p and q else HS_FACE
        perm = [
            ((a + p) * n_gy + b + q, a * n_gy + b)
            for a in range(n_gx) for b in range(n_gy)
            if 0 <= a + p < n_gx and 0 <= b + q < n_gy
        ]
        pieces.append(lax.ppermute(outgoing[:count], ("gx", "gy"), perm))
    smem = pl.BlockSpec(memory_space=pltpu.SMEM)
    vmem = pl.BlockSpec(memory_space=pltpu.VMEM)
    rates = pl.pallas_call(
        rates_kernel,
        out_shape=jax.ShapeDtypeStruct((TPD, 4, 128), f32),
        in_specs=[smem] * 3 + [vmem] * 9,
        out_specs=vmem,
        scratch_shapes=[
            pltpu.VMEM((7 * 3 * 64, 128), f32),
            pltpu.VMEM((EXT, 192, 128), bf16),
            pltpu.VMEM((2 * 3 * 64, 128), f32),
            pltpu.VMEM((TPD, 48, 128), f32),
            pltpu.VMEM((5, 128, 128), f32),
            pltpu.VMEM((EXT, 8, 128), f32),
            pltpu.SMEM((3 * TPD,), jnp.int32),
            pltpu.SMEM((3,), jnp.int32),
        ],
        compiler_params=pltpu.CompilerParams(vmem_limit_bytes=56 * 2**20),
    )(heavy_flag[0], order[0, 0], nbr[0, 0].reshape(-1), own, *pieces)
    return rates[None, None]


def solution(mesh):
    in_specs = (
        P("gx", "gy", None, None, None),
        P("gx", "gy"),
        P("gx", "gy", None),
        P("gx", "gy", None),
        P("gx", "gy", None, None),
    )
    out_specs = P("gx", "gy", None, None, None)
    return jax.shard_map(shards, mesh=mesh, in_specs=in_specs, out_specs=out_specs, check_vma=False)
```

```python
import math

import jax
import jax.numpy as jnp
from jax import lax
from jax.experimental import pallas as pl
from jax.experimental.pallas import tpu as pltpu
from jax.sharding import PartitionSpec as P

TPD = 256
NEIGHBOURS = 8
LIGHT = 128
HS_FACE = 64
HS_CORNER = 16
EXT = 576
OFFSETS = ((-1, -1), (-1, 0), (-1, 1), (0, -1), (0, 1), (1, -1), (1, 0), (1, 1))

SLOPE = -5.0 * 21.0 / (16.0 * math.pi)
ALPHA = 0.1 * math.sqrt(35.0) * 2.0
GAMMA = 2.0 / ALPHA
SOFT = 0.01 / 4.0
OWN_PART = (0, 0, 0, 1, 1, 2)
OTHER_PART = (0, 1, 2, 0, 1, 0)
BLOCKS = ((0, 0), (0, 1), (1, 0), (2, 0), (2, 1), (3, 0), (3, 1))
bf16, f32 = jnp.bfloat16, jnp.float32


def split3(v):
    hi = v.astype(bf16).astype(f32)
    rest = v - hi
    mid = rest.astype(bf16).astype(f32)
    return hi, mid, rest - mid


def fields(src, first):
    flat = src.reshape(src.shape[0] * 8, 128)

    def row(c):
        return flat[pl.ds(first * 8 + c, 8, stride=8), :]

    x, y, z = ((row(c) - 3.0) * 0.5 for c in range(3))
    u, v, w, rho, m = (row(c) for c in range(3, 8))
    r2 = rho * rho
    r4 = r2 * r2
    p = 5.0 * (r4 * r2 * rho - 1.0) / r2
    return x, y, z, u, v, w, rho, m, p, x * x + y * y + z * z, u * x + v * y + w * z


def other_rows(src, first):
    x, y, z, u, v, w, rho, m, p, xx, vx = fields(src, first)
    one = jnp.ones_like(x)
    gr = GAMMA * rho
    g2 = 2.0 * GAMMA
    return {
        (0, 3): 2.0 * x, (0, 4): 2.0 * y, (0, 5): 2.0 * z, (0, 7): xx, (0, 8): one,
        (1, 0): m * x, (1, 1): m * y, (1, 2): m * z, (1, 3): m * u, (1, 4): m * v, (1, 5): m * w,
        (1, 6): m, (1, 7): m * vx,
        (2, 3): 2.0 * gr * x, (2, 4): 2.0 * gr * y, (2, 5): 2.0 * gr * z, (2, 7): gr * (xx + SOFT), (2, 8): gr,
        (2, 9): g2 * x, (2, 10): g2 * y, (2, 11): g2 * z, (2, 12): GAMMA * one, (2, 13): GAMMA * xx,
        (3, 7): m * p, (3, 14): m,
    }


def own_rows(src, first):
    x, y, z, u, v, w, rho, m, p, xx, vx = fields(src, first)
    return (
        -u, -v, -w, -x, -y, -z, vx, jnp.ones_like(x),
        xx, -rho * x, -rho * y, -rho * z, rho * (xx + SOFT), rho, p,
    )


def other_tables(src, first, dest, stage, table, place):
    for (q, r), value in other_rows(src, first).items():
        b = BLOCKS.index((q, r // 8))
        for part, v in enumerate(split3(value)):
            stage[pl.ds(((b * 3 + part) * 8 + r % 8) * 8, 8), :] = v
    zero = jnp.zeros((8, 128), f32)
    for i in range(8):
        for part in range(3):
            for q in range(4):
                halves = [
                    stage[pl.ds((BLOCKS.index((q, h)) * 3 + part) * 64 + i, 8, stride=8), :]
                    if (q, h) in BLOCKS else zero
                    for h in range(2)
                ]
                at = part * 64 + q * 16
                table[dest + i, at:at + 16, :] = jnp.concatenate(halves, 0).astype(bf16)
        place[dest + i] = (src[first + i] - 3.0) * 0.5


def own_tables(src, first, stage, table):
    for r, value in enumerate(own_rows(src, first)):
        for part, v in enumerate(split3(value)):
            stage[pl.ds((((r // 8) * 3 + part) * 8 + r % 8) * 8, 8), :] = v
    for i in range(8):
        for part in range(3):
            for h in range(2):
                at = part * 16 + h * 8
                table[first + i, at:at + 8, :] = stage[pl.ds((h * 3 + part) * 64 + i, 8, stride=8), :]


def own_side(rows):
    parts = [rows[i * 16:(i + 1) * 16] for i in range(3)]
    return jnp.concatenate([parts[p] for p in OWN_PART], 0).T.astype(bf16)


def other_side(table, e):
    return jnp.concatenate(
        [
            jnp.concatenate([table[e, pl.ds(p * 64 + q * 16, 16), :] for p in OTHER_PART], 0)
            for q in range(4)
        ],
        1,
    )


def pair(own, other):
    g = jnp.dot(own, other, preferred_element_type=f32)
    h, c, d, a = (g[:, i * 128:(i + 1) * 128] for i in range(4))
    h = jnp.maximum(h, 1e-30)
    reach = jnp.maximum(1.0 - h * lax.rsqrt(h), 0.0)
    cube = reach * reach * reach
    push = (a - jnp.minimum(c, 0.0) * pl.reciprocal(d, approx=True)) * cube
    return push, cube * c


def tile_sums(own, entries, table, place):
    sums = None
    for e in entries:
        push, rate = pair(own, other_side(table, e))
        new = [push * place[e, 0:1], push * place[e, 1:2], push * place[e, 2:3], push, rate]
        sums = new if sums is None else [a + b for a, b in zip(sums, new)]
    return sums


def finish(acc, t, place, out):
    totals = [jnp.sum(acc[q].T, 0, keepdims=True) for q in range(5)]
    out[t, 0:3] = (-2.0 * SLOPE) * (place[t][:3] * totals[3] - jnp.concatenate(totals[:3], 0))
    out[t, 3:4] = (2.0 * SLOPE) * totals[4]


def rates_kernel(heavy, order, nbr, own, halo, out, stage, table, own_stage, own_table, acc, place, lists, counts):
    stage[...] = jnp.zeros_like(stage)
    own_stage[...] = jnp.zeros_like(own_stage)
    live = LIGHT + (TPD - LIGHT) * heavy[0]

    base = 0
    for src in (own, halo):
        def build(b, _, src=src, base=base):
            other_tables(src, b * 8, base + b * 8, stage, table, place)
            return 0

        lax.fori_loop(0, src.shape[0] // 8, build, 0)
        base += src.shape[0]

    def build_own(b, _):
        own_tables(own, b * 8, own_stage, own_table)
        return 0

    lax.fori_loop(0, TPD // 8, build_own, 0)

    for g in range(3):
        counts[g] = 0

    def sort(s, _):
        t = order[s]
        g = jnp.where(nbr[t * NEIGHBOURS + 6] >= 0, 1, 0) + jnp.where(nbr[t * NEIGHBOURS + 7] >= 0, 1, 0)
        n = counts[g]
        lists[g * TPD + n] = t
        counts[g] = n + 1
        return 0

    lax.fori_loop(0, live, sort, 0)

    def clear(s, _):
        out[order[s]] = jnp.zeros((4, 128), f32)
        return 0

    lax.fori_loop(live, TPD, clear, 0)

    for g in range(3):
        n = counts[g]

        def tile(s, mine, g=g, n=n):
            t = lists[g * TPD + s]
            finish(acc, lists[g * TPD + jnp.maximum(s - 1, 0)], place, out)
            following = own_side(own_table[lists[g * TPD + jnp.minimum(s + 1, n - 1)]])
            entries = [nbr[t * NEIGHBOURS + k] for k in range(6 + g)]
            for q, value in enumerate(tile_sums(mine, entries, table, place)):
                acc[q] = value
            return following

        @pl.when(n > 0)
        def _(tile=tile, g=g, n=n):
            lax.fori_loop(0, n, tile, own_side(own_table[lists[g * TPD]]))
            finish(acc, lists[g * TPD + n - 1], place, out)


def starts():
    first, at = [], 0
    for p, q in OFFSETS:
        first.append(at)
        at += HS_CORNER if p and q else HS_FACE
    return first, at


def exchange_kernel(n_gx, n_gy, send, own, halo, outgoing, send_sem, recv_sem):
    a, b = lax.axis_index("gx"), lax.axis_index("gy")
    first, _ = starts()

    def beside(p, q):
        inside = True
        for at, step, count in ((a, p, n_gx), (b, q, n_gy)):
            if step < 0:
                inside = inside & (at > 0)
            if step > 0:
                inside = inside & (at < count - 1)
        return inside

    barrier = pltpu.get_barrier_semaphore()
    for p, q in OFFSETS:
        @pl.when(beside(p, q))
        def _(p=p, q=q):
            pl.semaphore_signal(barrier, inc=1, device_id=(a + p, b + q), device_id_type=pl.DeviceIdType.MESH)

    def pick(s, _):
        outgoing[s] = own[send[s]]
        return 0

    lax.fori_loop(0, HS_FACE, pick, 0)
    rows = 1 + jnp.where(a > 0, 1, 0) + jnp.where(a < n_gx - 1, 1, 0)
    cols = 1 + jnp.where(b > 0, 1, 0) + jnp.where(b < n_gy - 1, 1, 0)
    pl.semaphore_wait(barrier, rows * cols - 1)

    def copy(i, there):
        p, q = OFFSETS[i]
        count = HS_CORNER if p and q else HS_FACE
        return pltpu.make_async_remote_copy(
            src_ref=outgoing.at[pl.ds(0, count)],
            dst_ref=halo.at[pl.ds(first[there], count)],
            send_sem=send_sem.at[i],
            recv_sem=recv_sem.at[there],
            device_id=(a + p, b + q),
            device_id_type=pl.DeviceIdType.MESH,
        )

    for i, (p, q) in enumerate(OFFSETS):
        @pl.when(beside(p, q))
        def _(i=i, p=p, q=q):
            copy(i, OFFSETS.index((-p, -q))).start()

    for i, (p, q) in enumerate(OFFSETS):
        count = HS_CORNER if p and q else HS_FACE

        @pl.when(jnp.logical_not(beside(p, q)))
        def _(i=i, count=count):
            halo[pl.ds(first[i], count)] = jnp.zeros((count, 8, 128), f32)

    for i, (p, q) in enumerate(OFFSETS):
        @pl.when(beside(p, q))
        def _(i=i, p=p, q=q):
            copy(i, OFFSETS.index((-p, -q))).wait_send()
            copy(i, i).wait_recv()


def exchange(own, send):
    vmem = pl.BlockSpec(memory_space=pltpu.VMEM)
    n_gx, n_gy = lax.axis_size("gx"), lax.axis_size("gy")

    def kernel(*refs):
        exchange_kernel(n_gx, n_gy, *refs)

    return pl.pallas_call(
        kernel,
        out_shape=jax.ShapeDtypeStruct((starts()[1], 8, 128), f32),
        in_specs=[pl.BlockSpec(memory_space=pltpu.SMEM), vmem],
        out_specs=vmem,
        scratch_shapes=[
            pltpu.VMEM((HS_FACE, 8, 128), f32),
            pltpu.SemaphoreType.DMA((8,)),
            pltpu.SemaphoreType.DMA((8,)),
        ],
        compiler_params=pltpu.CompilerParams(collective_id=0, has_side_effects=True, vmem_limit_bytes=8 * 2**20),
    )(send, own)


def shards(state, heavy_flag, order, send, nbr):
    own = state[0, 0]
    halo = exchange(own, send[0, 0])
    smem = pl.BlockSpec(memory_space=pltpu.SMEM)
    vmem = pl.BlockSpec(memory_space=pltpu.VMEM)
    rates = pl.pallas_call(
        rates_kernel,
        out_shape=jax.ShapeDtypeStruct((TPD, 4, 128), f32),
        in_specs=[smem] * 3 + [vmem] * 2,
        out_specs=vmem,
        scratch_shapes=[
            pltpu.VMEM((7 * 3 * 64, 128), f32),
            pltpu.VMEM((EXT, 192, 128), bf16),
            pltpu.VMEM((2 * 3 * 64, 128), f32),
            pltpu.VMEM((TPD, 48, 128), f32),
            pltpu.VMEM((5, 128, 128), f32),
            pltpu.VMEM((EXT, 8, 128), f32),
            pltpu.SMEM((3 * TPD,), jnp.int32),
            pltpu.SMEM((3,), jnp.int32),
        ],
        compiler_params=pltpu.CompilerParams(vmem_limit_bytes=56 * 2**20),
    )(heavy_flag[0], order[0, 0], nbr[0, 0].reshape(-1), own, halo)
    return rates[None, None]


def solution(mesh):
    in_specs = (
        P("gx", "gy", None, None, None),
        P("gx", "gy"),
        P("gx", "gy", None),
        P("gx", "gy", None),
        P("gx", "gy", None, None),
    )
    out_specs = P("gx", "gy", None, None, None)
    return jax.shard_map(shards, mesh=mesh, in_specs=in_specs, out_specs=out_specs, check_vma=False)
```

```python
import functools
import math

import jax
import jax.numpy as jnp
from jax import lax
from jax.experimental import pallas as pl
from jax.experimental.pallas import tpu as pltpu
from jax.sharding import PartitionSpec as P

TPD = 256
NEIGHBOURS = 8
LIGHT = 128
HS_FACE = 64
HS_CORNER = 16
EXT = 576
HELP = 44
OFFSETS = ((-1, -1), (-1, 0), (-1, 1), (0, -1), (0, 1), (1, -1), (1, 0), (1, 1))

SLOPE = -5.0 * 21.0 / (16.0 * math.pi)
ALPHA = 0.1 * math.sqrt(35.0) * 2.0
GAMMA = 2.0 / ALPHA
SOFT = 0.01 / 4.0
OWN_PART = (0, 0, 0, 1, 1, 2)
OTHER_PART = (0, 1, 2, 0, 1, 0)
BLOCKS = ((0, 0), (0, 1), (1, 0), (2, 0), (2, 1), (3, 0), (3, 1))
bf16, f32 = jnp.bfloat16, jnp.float32


def split3(v):
    hi = v.astype(bf16).astype(f32)
    rest = v - hi
    mid = rest.astype(bf16).astype(f32)
    return hi, mid, rest - mid


def fields(src, first):
    flat = src.reshape(src.shape[0] * 8, 128)

    def row(c):
        return flat[pl.ds(first * 8 + c, 8, stride=8), :]

    x, y, z = ((row(c) - 3.0) * 0.5 for c in range(3))
    u, v, w, rho, m = (row(c) for c in range(3, 8))
    r2 = rho * rho
    r4 = r2 * r2
    p = 5.0 * (r4 * r2 * rho - 1.0) / r2
    return x, y, z, u, v, w, rho, m, p, x * x + y * y + z * z, u * x + v * y + w * z


def other_rows(src, first):
    x, y, z, u, v, w, rho, m, p, xx, vx = fields(src, first)
    one = jnp.ones_like(x)
    gr = GAMMA * rho
    g2 = 2.0 * GAMMA
    return {
        (0, 3): 2.0 * x, (0, 4): 2.0 * y, (0, 5): 2.0 * z, (0, 7): xx, (0, 8): one,
        (1, 0): m * x, (1, 1): m * y, (1, 2): m * z, (1, 3): m * u, (1, 4): m * v, (1, 5): m * w,
        (1, 6): m, (1, 7): m * vx,
        (2, 3): 2.0 * gr * x, (2, 4): 2.0 * gr * y, (2, 5): 2.0 * gr * z, (2, 7): gr * (xx + SOFT), (2, 8): gr,
        (2, 9): g2 * x, (2, 10): g2 * y, (2, 11): g2 * z, (2, 12): GAMMA * one, (2, 13): GAMMA * xx,
        (3, 7): m * p, (3, 14): m,
    }


def own_rows(src, first):
    x, y, z, u, v, w, rho, m, p, xx, vx = fields(src, first)
    return (
        -u, -v, -w, -x, -y, -z, vx, jnp.ones_like(x),
        xx, -rho * x, -rho * y, -rho * z, rho * (xx + SOFT), rho, p,
    )


def other_tables(src, first, dest, stage, table, place):
    for (q, r), value in other_rows(src, first).items():
        b = BLOCKS.index((q, r // 8))
        for part, v in enumerate(split3(value)):
            stage[pl.ds(((b * 3 + part) * 8 + r % 8) * 8, 8), :] = v
    zero = jnp.zeros((8, 128), f32)
    for i in range(8):
        for part in range(3):
            for q in range(4):
                halves = [
                    stage[pl.ds((BLOCKS.index((q, h)) * 3 + part) * 64 + i, 8, stride=8), :]
                    if (q, h) in BLOCKS else zero
                    for h in range(2)
                ]
                at = part * 64 + q * 16
                table[dest + i, at:at + 16, :] = jnp.concatenate(halves, 0).astype(bf16)
        place[dest + i] = (src[first + i] - 3.0) * 0.5


def own_tables(src, first, stage, table):
    for r, value in enumerate(own_rows(src, first)):
        for part, v in enumerate(split3(value)):
            stage[pl.ds((((r // 8) * 3 + part) * 8 + r % 8) * 8, 8), :] = v
    for i in range(8):
        for part in range(3):
            for h in range(2):
                at = part * 16 + h * 8
                table[first + i, at:at + 8, :] = stage[pl.ds((h * 3 + part) * 64 + i, 8, stride=8), :]


def own_side(rows):
    parts = [rows[i * 16:(i + 1) * 16] for i in range(3)]
    return jnp.concatenate([parts[p] for p in OWN_PART], 0).T.astype(bf16)


def other_side(table, e):
    return jnp.concatenate(
        [
            jnp.concatenate([table[e, pl.ds(p * 64 + q * 16, 16), :] for p in OTHER_PART], 0)
            for q in range(4)
        ],
        1,
    )


def pair(own, other):
    g = jnp.dot(own, other, preferred_element_type=f32)
    h, c, d, a = (g[:, i * 128:(i + 1) * 128] for i in range(4))
    h = jnp.maximum(h, 1e-30)
    reach = jnp.maximum(1.0 - h * lax.rsqrt(h), 0.0)
    cube = reach * reach * reach
    push = (a - jnp.minimum(c, 0.0) * pl.reciprocal(d, approx=True)) * cube
    return push, cube * c


def tile_sums(own, entries, table, place):
    sums = None
    for e in entries:
        push, rate = pair(own, other_side(table, e))
        new = [push * place[e, 0:1], push * place[e, 1:2], push * place[e, 2:3], push, rate]
        sums = new if sums is None else [a + b for a, b in zip(sums, new)]
    return sums


def finish(acc, t, at, place, out):
    totals = [jnp.sum(acc[q].T, 0, keepdims=True) for q in range(5)]
    out[at, 0:3] = (-2.0 * SLOPE) * (place[t][:3] * totals[3] - jnp.concatenate(totals[:3], 0))
    out[at, 3:4] = (2.0 * SLOPE) * totals[4]


def rates_kernel(bounds, order, nbr, own, halo, out, stage, table, own_stage, own_table, acc, place, lists, counts, *, by_slot):
    low, high = bounds[0], bounds[1]

    @pl.when(high > low)
    def _():
        stage[...] = jnp.zeros_like(stage)
        base = 0
        for src in (own, halo):
            def build(b, _, src=src, base=base):
                other_tables(src, b * 8, base + b * 8, stage, table, place)
                return 0

            lax.fori_loop(0, src.shape[0] // 8, build, 0)
            base += src.shape[0]

        def build_own(b, _):
            own_tables(own, b * 8, own_stage, own_table)
            return 0

        own_stage[...] = jnp.zeros_like(own_stage)
        lax.fori_loop(0, TPD // 8, build_own, 0)

    for g in range(3):
        counts[g] = 0

    def sort(s, _):
        t = order[s]
        g = jnp.where(nbr[t * NEIGHBOURS + 6] >= 0, 1, 0) + jnp.where(nbr[t * NEIGHBOURS + 7] >= 0, 1, 0)
        n = counts[g]
        lists[0, g * TPD + n] = t
        lists[1, g * TPD + n] = s - low if by_slot else t
        counts[g] = n + 1
        return 0

    lax.fori_loop(low, high, sort, 0)

    def clear(s, _):
        out[order[s]] = jnp.zeros((4, 128), f32)
        return 0

    if not by_slot:
        lax.fori_loop(high, bounds[2], clear, 0)

    for g in range(3):
        n = counts[g]

        def tile(s, mine, g=g, n=n):
            t = lists[0, g * TPD + s]
            before = g * TPD + jnp.maximum(s - 1, 0)
            finish(acc, lists[0, before], lists[1, before], place, out)
            following = own_side(own_table[lists[0, g * TPD + jnp.minimum(s + 1, n - 1)]])
            entries = [nbr[t * NEIGHBOURS + k] for k in range(6 + g)]
            for q, value in enumerate(tile_sums(mine, entries, table, place)):
                acc[q] = value
            return following

        @pl.when(n > 0)
        def _(tile=tile, g=g, n=n):
            lax.fori_loop(0, n, tile, own_side(own_table[lists[0, g * TPD]]))
            last = g * TPD + n - 1
            finish(acc, lists[0, last], lists[1, last], place, out)


def rates_of(bounds, order, nbr, own, halo, count, by_slot):
    smem = pl.BlockSpec(memory_space=pltpu.SMEM)
    vmem = pl.BlockSpec(memory_space=pltpu.VMEM)
    return pl.pallas_call(
        functools.partial(rates_kernel, by_slot=by_slot),
        out_shape=jax.ShapeDtypeStruct((count, 4, 128), f32),
        in_specs=[smem] * 3 + [vmem] * 2,
        out_specs=vmem,
        scratch_shapes=[
            pltpu.VMEM((7 * 3 * 64, 128), f32),
            pltpu.VMEM((EXT, 192, 128), bf16),
            pltpu.VMEM((2 * 3 * 64, 128), f32),
            pltpu.VMEM((TPD, 48, 128), f32),
            pltpu.VMEM((5, 128, 128), f32),
            pltpu.VMEM((EXT, 8, 128), f32),
            pltpu.SMEM((2, 3 * TPD), jnp.int32),
            pltpu.SMEM((3,), jnp.int32),
        ],
        compiler_params=pltpu.CompilerParams(vmem_limit_bytes=56 * 2**20),
        cost_estimate=pl.CostEstimate(flops=count * 8 * 128 * 128 * 1000, bytes_accessed=4 * 2**20, transcendentals=0),
    )(bounds, order, nbr, own, halo)


def merge_kernel(heavy, order, mine, helped, out):
    out[...] = mine[...]

    def put(s, _):
        out[order[TPD - HELP + s]] = helped[s]
        return 0

    lax.fori_loop(0, HELP * heavy[0], put, 0)


def merge(heavy, order, mine, helped):
    smem = pl.BlockSpec(memory_space=pltpu.SMEM)
    vmem = pl.BlockSpec(memory_space=pltpu.VMEM)
    return pl.pallas_call(
        merge_kernel,
        out_shape=jax.ShapeDtypeStruct((TPD, 4, 128), f32),
        in_specs=[smem] * 2 + [vmem] * 2,
        out_specs=vmem,
    )(heavy, order, mine, helped)


def starts():
    first, at = [], 0
    for p, q in OFFSETS:
        first.append(at)
        at += HS_CORNER if p and q else HS_FACE
    return first, at


def exchange_kernel(n_gx, n_gy, send, own, halo, outgoing, send_sem, recv_sem):
    a, b = lax.axis_index("gx"), lax.axis_index("gy")
    first, _ = starts()

    def beside(p, q):
        inside = True
        for at, step, count in ((a, p, n_gx), (b, q, n_gy)):
            if step < 0:
                inside = inside & (at > 0)
            if step > 0:
                inside = inside & (at < count - 1)
        return inside

    barrier = pltpu.get_barrier_semaphore()
    for p, q in OFFSETS:
        @pl.when(beside(p, q))
        def _(p=p, q=q):
            pl.semaphore_signal(barrier, inc=1, device_id=(a + p, b + q), device_id_type=pl.DeviceIdType.MESH)

    def pick(s, _):
        outgoing[s] = own[send[s]]
        return 0

    lax.fori_loop(0, HS_FACE, pick, 0)
    rows = 1 + jnp.where(a > 0, 1, 0) + jnp.where(a < n_gx - 1, 1, 0)
    cols = 1 + jnp.where(b > 0, 1, 0) + jnp.where(b < n_gy - 1, 1, 0)
    pl.semaphore_wait(barrier, rows * cols - 1)

    def copy(i, there):
        p, q = OFFSETS[i]
        count = HS_CORNER if p and q else HS_FACE
        return pltpu.make_async_remote_copy(
            src_ref=outgoing.at[pl.ds(0, count)],
            dst_ref=halo.at[pl.ds(first[there], count)],
            send_sem=send_sem.at[i],
            recv_sem=recv_sem.at[there],
            device_id=(a + p, b + q),
            device_id_type=pl.DeviceIdType.MESH,
        )

    for i, (p, q) in enumerate(OFFSETS):
        @pl.when(beside(p, q))
        def _(i=i, p=p, q=q):
            copy(i, OFFSETS.index((-p, -q))).start()

    for i, (p, q) in enumerate(OFFSETS):
        count = HS_CORNER if p and q else HS_FACE

        @pl.when(jnp.logical_not(beside(p, q)))
        def _(i=i, count=count):
            halo[pl.ds(first[i], count)] = jnp.zeros((count, 8, 128), f32)

    for i, (p, q) in enumerate(OFFSETS):
        @pl.when(beside(p, q))
        def _(i=i, p=p, q=q):
            copy(i, OFFSETS.index((-p, -q))).wait_send()
            copy(i, i).wait_recv()


def exchange(own, send):
    vmem = pl.BlockSpec(memory_space=pltpu.VMEM)
    n_gx, n_gy = lax.axis_size("gx"), lax.axis_size("gy")

    def kernel(*refs):
        exchange_kernel(n_gx, n_gy, *refs)

    return pl.pallas_call(
        kernel,
        out_shape=jax.ShapeDtypeStruct((starts()[1], 8, 128), f32),
        in_specs=[pl.BlockSpec(memory_space=pltpu.SMEM), vmem],
        out_specs=vmem,
        scratch_shapes=[
            pltpu.VMEM((HS_FACE, 8, 128), f32),
            pltpu.SemaphoreType.DMA((8,)),
            pltpu.SemaphoreType.DMA((8,)),
        ],
        compiler_params=pltpu.CompilerParams(collective_id=0, has_side_effects=True, vmem_limit_bytes=8 * 2**20),
    )(send, own)


def shards(state, heavy_flag, order, send, nbr):
    own, order, nbr = state[0, 0], order[0, 0], nbr[0, 0].reshape(-1)
    heavy = heavy_flag[0]
    half = lax.axis_size("gx") // 2
    partners = [(g, (g + half) % (2 * half)) for g in range(2 * half)]
    halo = exchange(own, send[0, 0])
    own_out, halo_out, lists = lax.optimization_barrier((own, halo, jnp.concatenate([order, nbr])))
    far_own, far_halo, far_lists = (lax.ppermute(v, "gx", partners) for v in (own_out, halo_out, lists))
    live = LIGHT + (TPD - HELP - LIGHT) * heavy
    bounds = jnp.concatenate([jnp.zeros_like(live), live, jnp.where(heavy > 0, live, TPD)])
    mine = rates_of(bounds, order, nbr, own, halo, TPD, False)
    far_bounds = jnp.concatenate([TPD - HELP * (1 - heavy), jnp.full_like(live, TPD), jnp.full_like(live, TPD)])
    far_bounds, mine = lax.optimization_barrier((far_bounds, mine))
    helped = rates_of(far_bounds, far_lists[:TPD], far_lists[TPD:], far_own, far_halo, HELP, True)
    helped = lax.ppermute(helped, "gx", partners)
    return merge(heavy, order, mine, helped)[None, None]


def solution(mesh):
    in_specs = (
        P("gx", "gy", None, None, None),
        P("gx", "gy"),
        P("gx", "gy", None),
        P("gx", "gy", None),
        P("gx", "gy", None, None),
    )
    out_specs = P("gx", "gy", None, None, None)
    return jax.shard_map(shards, mesh=mesh, in_specs=in_specs, out_specs=out_specs, check_vma=False)
```

```python
import functools
import math

import jax
import jax.numpy as jnp
from jax import lax
from jax.experimental import pallas as pl
from jax.experimental.pallas import tpu as pltpu
from jax.sharding import PartitionSpec as P

TPD = 256
NEIGHBOURS = 8
LIGHT = 128
HS_FACE = 64
HS_CORNER = 16
EXT = 576
HELP = 40
OFFSETS = ((-1, -1), (-1, 0), (-1, 1), (0, -1), (0, 1), (1, -1), (1, 0), (1, 1))

SLOPE = -5.0 * 21.0 / (16.0 * math.pi)
ALPHA = 0.1 * math.sqrt(35.0) * 2.0
GAMMA = 2.0 / ALPHA
SOFT = 0.01 / 4.0
OWN_PART = (0, 0, 0, 1, 1, 2)
OTHER_PART = (0, 1, 2, 0, 1, 0)
BLOCKS = ((0, 0), (0, 1), (1, 0), (2, 0), (2, 1), (3, 0), (3, 1))
SIDE = 4
STAGE = 7 * 3 * 64
bf16, f32 = jnp.bfloat16, jnp.float32


def split3(v):
    hi = v.astype(bf16).astype(f32)
    rest = v - hi
    mid = rest.astype(bf16).astype(f32)
    return hi, mid, rest - mid


def fields(src, first):
    flat = src.reshape(src.shape[0] * 8, 128)

    def row(c):
        return flat[pl.ds(first * 8 + c, 8, stride=8), :]

    x, y, z = ((row(c) - 3.0) * 0.5 for c in range(3))
    u, v, w, rho, m = (row(c) for c in range(3, 8))
    r2 = rho * rho
    r4 = r2 * r2
    p = 5.0 * (r4 * r2 * rho - 1.0) / r2
    return x, y, z, u, v, w, rho, m, p, x * x + y * y + z * z, u * x + v * y + w * z


def other_rows(src, first):
    x, y, z, u, v, w, rho, m, p, xx, vx = fields(src, first)
    one = jnp.ones_like(x)
    gr = GAMMA * rho
    g2 = 2.0 * GAMMA
    return {
        (0, 3): 2.0 * x, (0, 4): 2.0 * y, (0, 5): 2.0 * z, (0, 7): xx, (0, 8): one,
        (1, 0): m * x, (1, 1): m * y, (1, 2): m * z, (1, 3): m * u, (1, 4): m * v, (1, 5): m * w,
        (1, 6): m, (1, 7): m * vx,
        (2, 3): 2.0 * gr * x, (2, 4): 2.0 * gr * y, (2, 5): 2.0 * gr * z, (2, 7): gr * (xx + SOFT), (2, 8): gr,
        (2, 9): g2 * x, (2, 10): g2 * y, (2, 11): g2 * z, (2, 12): GAMMA * one, (2, 13): GAMMA * xx,
        (3, 7): m * p, (3, 14): m,
    }


def own_rows(src, first):
    x, y, z, u, v, w, rho, m, p, xx, vx = fields(src, first)
    return (
        -u, -v, -w, -x, -y, -z, vx, jnp.ones_like(x),
        xx, -rho * x, -rho * y, -rho * z, rho * (xx + SOFT), rho, p,
    )


def stage_rows(src, first, stage, at):
    for (q, r), value in other_rows(src, first).items():
        b = BLOCKS.index((q, r // 8))
        for part, v in enumerate(split3(value)):
            stage[pl.ds(at + ((b * 3 + part) * 8 + r % 8) * 8, 8), :] = v


def store_tables(src, first, dest, stage, at, table, place):
    zero = jnp.zeros((8, 128), f32)
    for i in range(8):
        for part in range(3):
            for q in range(4):
                halves = [
                    stage[pl.ds(at + (BLOCKS.index((q, h)) * 3 + part) * 64 + i, 8, stride=8), :]
                    if (q, h) in BLOCKS else zero
                    for h in range(2)
                ]
                row = part * 64 + q * 16
                table[dest + i, row:row + 16, :] = jnp.concatenate(halves, 0).astype(bf16)
        place[dest + i] = (src[first + i] - 3.0) * 0.5


def own_tables(src, first, stage, table):
    for r, value in enumerate(own_rows(src, first)):
        for part, v in enumerate(split3(value)):
            stage[pl.ds((((r // 8) * 3 + part) * 8 + r % 8) * 8, 8), :] = v
    for i in range(8):
        for part in range(3):
            for h in range(2):
                at = part * 16 + h * 8
                table[first + i, at:at + 8, :] = stage[pl.ds((h * 3 + part) * 64 + i, 8, stride=8), :]


def own_side(rows):
    parts = [rows[i * 16:(i + 1) * 16] for i in range(3)]
    return jnp.concatenate([parts[p] for p in OWN_PART], 0).T.astype(bf16)


def other_side(table, e):
    return jnp.concatenate(
        [
            jnp.concatenate([table[e, pl.ds(p * 64 + q * 16, 16), :] for p in OTHER_PART], 0)
            for q in range(4)
        ],
        1,
    )


def pair(own, other):
    g = jnp.dot(own, other, preferred_element_type=f32)
    h, c, d, a = (g[:, i * 128:(i + 1) * 128] for i in range(4))
    h = jnp.maximum(h, 1e-30)
    reach = jnp.maximum(1.0 - h * lax.rsqrt(h), 0.0)
    cube = reach * reach * reach
    push = (a - jnp.minimum(c, 0.0) * pl.reciprocal(d, approx=True)) * cube
    return push, cube * c


def tile_sums(own, entries, table, place):
    sums = None
    for e in entries:
        push, rate = pair(own, other_side(table, e))
        new = [push * place[e, 0:1], push * place[e, 1:2], push * place[e, 2:3], push, rate]
        sums = new if sums is None else [a + b for a, b in zip(sums, new)]
    return sums


def finish(acc, t, at, place, out):
    totals = [jnp.sum(acc[q].T, 0, keepdims=True) for q in range(5)]
    out[at, 0:3] = (-2.0 * SLOPE) * (place[t][:3] * totals[3] - jnp.concatenate(totals[:3], 0))
    out[at, 3:4] = (2.0 * SLOPE) * totals[4]


def rates_kernel(bounds, order, nbr, ext, out, stage, table, own_stage, own_table, acc, place, lists, blank, sides, *, by_slot):
    low, high = bounds[0], bounds[1]

    @pl.when(high > low)
    def _():
        stage[...] = jnp.zeros_like(stage)
        own_stage[...] = jnp.zeros_like(own_stage)
        blank[...] = jnp.where(lax.broadcasted_iota(jnp.int32, blank.shape, 1) == 6, 1.0, 0.0)

        def build(b, _):
            for i in range(2):
                stage_rows(ext, b * 16 + i * 8, stage, i * STAGE)
            for i in range(2):
                store_tables(ext, b * 16 + i * 8, b * 16 + i * 8, stage, i * STAGE, table, place)
            return 0

        lax.fori_loop(0, EXT // 16, build, 0)
        stage_rows(blank, 0, stage, 0)
        store_tables(blank, 0, EXT, stage, 0, table, place)

        def build_own(b, _):
            own_tables(ext, b * 8, own_stage, own_table)
            return 0

        lax.fori_loop(0, TPD // 8, build_own, 0)

    def sort(b, sizes):
        for i in range(4):
            s = low + b * 4 + i
            t = order[s]
            seven = nbr[t * NEIGHBOURS + 6] >= 0
            eight = nbr[t * NEIGHBOURS + 7] >= 0
            n = jnp.where(eight, sizes[2], jnp.where(seven, sizes[1], sizes[0]))
            at = n + jnp.where(eight, 2 * TPD, jnp.where(seven, TPD, 0))
            lists[0, at] = t
            lists[1, at] = s - low if by_slot else t
            sizes = (
                jnp.where(seven, sizes[0], sizes[0] + 1),
                jnp.where(eight, sizes[1], jnp.where(seven, sizes[1] + 1, sizes[1])),
                jnp.where(eight, sizes[2] + 1, sizes[2]),
            )
        return sizes

    none = jnp.int32(0)
    sizes = list(lax.fori_loop(0, (high - low) // 4, sort, (none, none, none)))

    for g in range(2):
        odd = lax.rem(sizes[g], SIDE)
        for i in range(SIDE - 1):
            @pl.when(i < odd)
            def _(g=g, i=i):
                for c in range(2):
                    lists[c, (g + 1) * TPD + sizes[g + 1] + i] = lists[c, g * TPD + sizes[g] - 1 - i]
        sizes[g] = sizes[g] - odd
        sizes[g + 1] = sizes[g + 1] + odd

    def clear(s, _):
        out[order[s]] = jnp.zeros((4, 128), f32)
        return 0

    if not by_slot:
        lax.fori_loop(high, bounds[2], clear, 0)

    for g in range(3):
        n = sizes[g]
        steps = lax.div(n + SIDE - 1, SIDE)

        def look(s, g=g, n=n):
            found = []
            for i in range(SIDE):
                at = g * TPD + jnp.clip(s * SIDE + i, 0, n - 1)
                t = lists[0, at]
                entries = [nbr[t * NEIGHBOURS + k] for k in range(6 + g)]
                entries = [jnp.where(e < 0, EXT, e) for e in entries]
                found.append((t, lists[1, at], *entries))
            return tuple(found)

        def step(s, carried, look=look):
            before, now = carried
            following = look(s + 1)
            mine = [sides[i] for i in range(SIDE)]
            for i in range(SIDE):
                finish(acc.at[pl.ds(5 * i, 5)], before[i][0], before[i][1], place, out)
            for i in range(SIDE):
                for q, value in enumerate(tile_sums(mine[i], now[i][2:], table, place)):
                    acc[5 * i + q] = value
            for i in range(SIDE):
                sides[i] = own_side(own_table[following[i][0]])
            return tuple(x[:2] for x in now), following

        @pl.when(n > 0)
        def _(look=look, step=step, steps=steps):
            first = look(0)
            for i in range(SIDE):
                sides[i] = own_side(own_table[first[i][0]])
            before, _ = lax.fori_loop(0, steps, step, (tuple(x[:2] for x in first), first))
            for i in range(SIDE):
                finish(acc.at[pl.ds(5 * i, 5)], before[i][0], before[i][1], place, out)


def rates_of(bounds, order, nbr, ext, count, by_slot):
    smem = pl.BlockSpec(memory_space=pltpu.SMEM)
    vmem = pl.BlockSpec(memory_space=pltpu.VMEM)
    return pl.pallas_call(
        functools.partial(rates_kernel, by_slot=by_slot),
        out_shape=jax.ShapeDtypeStruct((count, 4, 128), f32),
        in_specs=[smem] * 3 + [vmem],
        out_specs=vmem,
        scratch_shapes=[
            pltpu.VMEM((2 * STAGE, 128), f32),
            pltpu.VMEM((EXT + 8, 192, 128), bf16),
            pltpu.VMEM((2 * 3 * 64, 128), f32),
            pltpu.VMEM((TPD, 48, 128), f32),
            pltpu.VMEM((5 * SIDE, 128, 128), f32),
            pltpu.VMEM((EXT + 8, 8, 128), f32),
            pltpu.SMEM((2, 3 * TPD + SIDE), jnp.int32),
            pltpu.VMEM((8, 8, 128), f32),
            pltpu.VMEM((SIDE, 128, 96), bf16),
        ],
        compiler_params=pltpu.CompilerParams(vmem_limit_bytes=56 * 2**20),
        cost_estimate=pl.CostEstimate(flops=count * 8 * 128 * 128 * 1000, bytes_accessed=4 * 2**20, transcendentals=0),
    )(bounds, order, nbr, ext)


def merge_kernel(heavy, order, mine, helped, out):
    out[...] = mine[...]

    def put(s, _):
        out[order[TPD - HELP + s]] = helped[s]
        return 0

    lax.fori_loop(0, HELP * heavy[0], put, 0)


def merge(heavy, order, mine, helped):
    smem = pl.BlockSpec(memory_space=pltpu.SMEM)
    vmem = pl.BlockSpec(memory_space=pltpu.VMEM)
    return pl.pallas_call(
        merge_kernel,
        out_shape=jax.ShapeDtypeStruct((TPD, 4, 128), f32),
        in_specs=[smem] * 2 + [vmem] * 2,
        out_specs=vmem,
    )(heavy, order, mine, helped)


def starts():
    first, at = [], TPD
    for p, q in OFFSETS:
        first.append(at)
        at += HS_CORNER if p and q else HS_FACE
    return first, at


def exchange_kernel(n_gx, n_gy, send, own, ext, outgoing, send_sem, recv_sem):
    a, b = lax.axis_index("gx"), lax.axis_index("gy")
    first, _ = starts()

    def beside(p, q):
        inside = True
        for at, step, count in ((a, p, n_gx), (b, q, n_gy)):
            if step < 0:
                inside = inside & (at > 0)
            if step > 0:
                inside = inside & (at < count - 1)
        return inside

    barrier = pltpu.get_barrier_semaphore()
    for p, q in OFFSETS:
        @pl.when(beside(p, q))
        def _(p=p, q=q):
            pl.semaphore_signal(barrier, inc=1, device_id=(a + p, b + q), device_id_type=pl.DeviceIdType.MESH)

    def pick(s, _):
        outgoing[s] = own[send[s]]
        return 0

    lax.fori_loop(0, HS_FACE, pick, 0)
    rows = 1 + jnp.where(a > 0, 1, 0) + jnp.where(a < n_gx - 1, 1, 0)
    cols = 1 + jnp.where(b > 0, 1, 0) + jnp.where(b < n_gy - 1, 1, 0)
    pl.semaphore_wait(barrier, rows * cols - 1)

    def copy(i, there):
        p, q = OFFSETS[i]
        count = HS_CORNER if p and q else HS_FACE
        return pltpu.make_async_remote_copy(
            src_ref=outgoing.at[pl.ds(0, count)],
            dst_ref=ext.at[pl.ds(first[there], count)],
            send_sem=send_sem.at[i],
            recv_sem=recv_sem.at[there],
            device_id=(a + p, b + q),
            device_id_type=pl.DeviceIdType.MESH,
        )

    for i, (p, q) in enumerate(OFFSETS):
        @pl.when(beside(p, q))
        def _(i=i, p=p, q=q):
            copy(i, OFFSETS.index((-p, -q))).start()

    def keep(b, _):
        ext[pl.ds(b * 8, 8)] = own[pl.ds(b * 8, 8)]
        return 0

    lax.fori_loop(0, TPD // 8, keep, 0)
    for i, (p, q) in enumerate(OFFSETS):
        count = HS_CORNER if p and q else HS_FACE

        @pl.when(jnp.logical_not(beside(p, q)))
        def _(i=i, count=count):
            ext[pl.ds(first[i], count)] = jnp.zeros((count, 8, 128), f32)

    for i, (p, q) in enumerate(OFFSETS):
        @pl.when(beside(p, q))
        def _(i=i, p=p, q=q):
            copy(i, OFFSETS.index((-p, -q))).wait_send()
            copy(i, i).wait_recv()


def exchange(own, send):
    vmem = pl.BlockSpec(memory_space=pltpu.VMEM)
    n_gx, n_gy = lax.axis_size("gx"), lax.axis_size("gy")

    def kernel(*refs):
        exchange_kernel(n_gx, n_gy, *refs)

    return pl.pallas_call(
        kernel,
        out_shape=jax.ShapeDtypeStruct((starts()[1], 8, 128), f32),
        in_specs=[pl.BlockSpec(memory_space=pltpu.SMEM), vmem],
        out_specs=vmem,
        scratch_shapes=[
            pltpu.VMEM((HS_FACE, 8, 128), f32),
            pltpu.SemaphoreType.DMA((8,)),
            pltpu.SemaphoreType.DMA((8,)),
        ],
        compiler_params=pltpu.CompilerParams(collective_id=0, has_side_effects=True, vmem_limit_bytes=8 * 2**20),
    )(send, own)


def shards(state, heavy_flag, order, send, nbr):
    own, order, nbr = state[0, 0], order[0, 0], nbr[0, 0].reshape(-1)
    heavy = heavy_flag[0]
    half = lax.axis_size("gx") // 2
    partners = [(g, (g + half) % (2 * half)) for g in range(2 * half)]
    ext = exchange(own, send[0, 0])
    ext_out, lists = lax.optimization_barrier((ext, jnp.concatenate([order, nbr])))
    far_ext, far_lists = (lax.ppermute(v, "gx", partners) for v in (ext_out, lists))
    live = LIGHT + (TPD - HELP - LIGHT) * heavy
    bounds = jnp.concatenate([jnp.zeros_like(live), live, jnp.where(heavy > 0, live, TPD)])
    mine = rates_of(bounds, order, nbr, ext, TPD, False)
    far_bounds = jnp.concatenate([TPD - HELP * (1 - heavy), jnp.full_like(live, TPD), jnp.full_like(live, TPD)])
    far_bounds, mine = lax.optimization_barrier((far_bounds, mine))
    helped = rates_of(far_bounds, far_lists[:TPD], far_lists[TPD:], far_ext, HELP, True)
    helped = lax.ppermute(helped, "gx", partners)
    return merge(heavy, order, mine, helped)[None, None]


def solution(mesh):
    in_specs = (
        P("gx", "gy", None, None, None),
        P("gx", "gy"),
        P("gx", "gy", None),
        P("gx", "gy", None),
        P("gx", "gy", None, None),
    )
    out_specs = P("gx", "gy", None, None, None)
    return jax.shard_map(shards, mesh=mesh, in_specs=in_specs, out_specs=out_specs, check_vma=False)
```

```python
import functools
import math

import jax
import jax.numpy as jnp
from jax import lax
from jax.experimental import pallas as pl
from jax.experimental.pallas import tpu as pltpu
from jax.sharding import PartitionSpec as P

TPD = 256
NEIGHBOURS = 8
LIGHT = 128
HS_FACE = 64
HS_CORNER = 16
EXT = 576
HELP = 48
OFFSETS = ((-1, -1), (-1, 0), (-1, 1), (0, -1), (0, 1), (1, -1), (1, 0), (1, 1))

SLOPE = -5.0 * 21.0 / (16.0 * math.pi)
ALPHA = 0.1 * math.sqrt(35.0) * 2.0
GAMMA = 2.0 / ALPHA
SOFT = 0.01 / 4.0
OWN_PART = (0, 0, 0, 1, 1, 2)
OTHER_PART = (0, 1, 2, 0, 1, 0)
BLOCKS = ((0, 0), (1, 0), (2, 0), (2, 1))
SIDE = 4
STAGE = 5 * 64
bf16, f32 = jnp.bfloat16, jnp.float32


def split3(v):
    hi = v.astype(bf16).astype(f32)
    rest = v - hi
    mid = rest.astype(bf16).astype(f32)
    return hi, mid, rest - mid


def fields(src, first):
    flat = src.reshape(src.shape[0] * 8, 128)

    def row(c):
        return flat[pl.ds(first * 8 + c, 8, stride=8), :]

    x, y, z = ((row(c) - 3.0) * 0.5 for c in range(3))
    u, v, w, rho, m = (row(c) for c in range(3, 8))
    r2 = rho * rho
    r4 = r2 * r2
    p = 5.0 * (r4 * r2 * rho - 1.0) / r2
    return x, y, z, u, v, w, rho, m, p, x * x + y * y + z * z, u * x + v * y + w * z


def other_rows(src, first):
    x, y, z, u, v, w, rho, m, p, xx, vx = fields(src, first)
    one = jnp.ones_like(x)
    gr = GAMMA * rho
    g2 = 2.0 * GAMMA
    return {
        (0, 3): 2.0 * x, (0, 4): 2.0 * y, (0, 5): 2.0 * z, (0, 7): xx,
        (1, 0): m * x, (1, 1): m * y, (1, 2): m * z, (1, 3): m * u, (1, 4): m * v, (1, 5): m * w,
        (1, 6): m, (1, 7): m * vx,
        (2, 3): 2.0 * gr * x, (2, 4): 2.0 * gr * y, (2, 5): 2.0 * gr * z, (2, 7): gr * (xx + SOFT), (2, 8): gr,
        (2, 9): g2 * x, (2, 10): g2 * y, (2, 11): g2 * z, (2, 12): GAMMA * one, (2, 13): GAMMA * xx,
        (3, 7): m * p, (3, 6): m,
    }


def own_rows(src, first):
    x, y, z, u, v, w, rho, m, p, xx, vx = fields(src, first)
    return (
        -u, -v, -w, -x, -y, -z, vx, jnp.ones_like(x),
        xx, -rho * x, -rho * y, -rho * z, rho * (xx + SOFT), rho, p,
    )


def stage_rows(src, first, stage, at):
    for (q, r), value in other_rows(src, first).items():
        b, i = (len(BLOCKS), r) if q == 3 else (BLOCKS.index((q, r // 8)), r % 8)
        stage[pl.ds(at + (b * 8 + i) * 8, 8), :] = value


def store_tables(src, first, dest, stage, at, table, place):
    zero = jnp.zeros((8, 128), f32)
    row = lax.broadcasted_iota(jnp.int32, (8, 128), 0)
    one = jnp.where(row == 0, 1.0, 0.0)
    for i in range(8):
        blocks = [split3(stage[pl.ds(at + b * 64 + i, 8, stride=8), :]) for b in range(len(BLOCKS) + 1)]
        for part in range(3):
            h, c, d, d_end, a = (block[part] for block in blocks)
            halves = (
                (h, zero if part else one),
                (c, zero),
                (d, d_end),
                (jnp.where(row == 7, a, 0.0), jnp.where(row == 6, a, 0.0)),
            )
            for q in range(4):
                to = part * 64 + q * 16
                table[dest + i, to:to + 16, :] = jnp.concatenate(halves[q], 0).astype(bf16)
        place[dest + i] = (src[first + i] - 3.0) * 0.5


def own_tables(src, first, stage, table):
    for r, value in enumerate(own_rows(src, first)):
        stage[pl.ds(r * 8, 8), :] = value
    for i in range(8):
        for h in range(2):
            for part, v in enumerate(split3(stage[pl.ds(h * 64 + i, 8, stride=8), :])):
                at = part * 16 + h * 8
                table[first + i, at:at + 8, :] = v


def own_side(rows):
    parts = [rows[i * 16:(i + 1) * 16] for i in range(3)]
    return jnp.concatenate([parts[p] for p in OWN_PART], 0).T.astype(bf16)


def other_side(table, e):
    return jnp.concatenate(
        [
            jnp.concatenate([table[e, pl.ds(p * 64 + q * 16, 16), :] for p in OTHER_PART], 0)
            for q in range(4)
        ],
        1,
    )


def pair(own, other):
    g = jnp.dot(own, other, preferred_element_type=f32)
    h, c, d, a = (g[:, i * 128:(i + 1) * 128] for i in range(4))
    h = jnp.maximum(h, 1e-30)
    reach = jnp.maximum(1.0 - h * lax.rsqrt(h), 0.0)
    cube = reach * reach * reach
    push = (a - jnp.minimum(c, 0.0) * pl.reciprocal(d, approx=True)) * cube
    return push, cube * c


def tile_sums(own, entries, table, place):
    sums = None
    for e in entries:
        push, rate = pair(own, other_side(table, e))
        new = [push * place[e, 0:1], push * place[e, 1:2], push * place[e, 2:3], push, rate]
        sums = new if sums is None else [a + b for a, b in zip(sums, new)]
    return sums


def finish(acc, t, at, place, out):
    totals = [jnp.sum(acc[q].T, 0, keepdims=True) for q in range(5)]
    out[at, 0:3] = (-2.0 * SLOPE) * (place[t][:3] * totals[3] - jnp.concatenate(totals[:3], 0))
    out[at, 3:4] = (2.0 * SLOPE) * totals[4]


def rates_kernel(bounds, order, nbr, source, out, ext, stage, table, own_stage, own_table, acc, place, lists, blank, sides, sem, *, by_slot):
    low, high = bounds[0], bounds[1]

    @pl.when(high > low)
    def _():
        fetch = pltpu.make_async_copy(source, ext, sem)
        fetch.start()
        stage[...] = jnp.zeros_like(stage)
        own_stage[...] = jnp.zeros_like(own_stage)
        blank[...] = jnp.where(lax.broadcasted_iota(jnp.int32, blank.shape, 1) == 6, 1.0, 0.0)

        fetch.wait()

        def build(b, _):
            stage_rows(ext, b * 16 + 8, stage, STAGE)
            store_tables(ext, b * 16, b * 16, stage, 0, table, place)
            stage_rows(ext, jnp.minimum(b * 16 + 16, EXT - 8), stage, 0)
            store_tables(ext, b * 16 + 8, b * 16 + 8, stage, STAGE, table, place)
            return 0

        stage_rows(ext, 0, stage, 0)
        lax.fori_loop(0, EXT // 16, build, 0)
        stage_rows(blank, 0, stage, 0)
        store_tables(blank, 0, EXT, stage, 0, table, place)

        def build_own(b, _):
            own_tables(ext, b * 8, own_stage, own_table)
            return 0

        lax.fori_loop(0, TPD // 8, build_own, 0)

    def sort(b, sizes):
        for i in range(4):
            s = low + b * 4 + i
            t = order[s]
            seven = nbr[t * NEIGHBOURS + 6] >= 0
            eight = nbr[t * NEIGHBOURS + 7] >= 0
            n = jnp.where(eight, sizes[2], jnp.where(seven, sizes[1], sizes[0]))
            at = n + jnp.where(eight, 2 * TPD, jnp.where(seven, TPD, 0))
            lists[0, at] = t
            lists[1, at] = s - low if by_slot else t
            sizes = (
                jnp.where(seven, sizes[0], sizes[0] + 1),
                jnp.where(eight, sizes[1], jnp.where(seven, sizes[1] + 1, sizes[1])),
                jnp.where(eight, sizes[2] + 1, sizes[2]),
            )
        return sizes

    none = jnp.int32(0)
    sizes = list(lax.fori_loop(0, (high - low) // 4, sort, (none, none, none)))

    for g in range(2):
        odd = lax.rem(sizes[g], SIDE)
        for i in range(SIDE - 1):
            @pl.when(i < odd)
            def _(g=g, i=i):
                for c in range(2):
                    lists[c, (g + 1) * TPD + sizes[g + 1] + i] = lists[c, g * TPD + sizes[g] - 1 - i]
        sizes[g] = sizes[g] - odd
        sizes[g + 1] = sizes[g + 1] + odd

    def clear(s, _):
        out[order[s]] = jnp.zeros((4, 128), f32)
        return 0

    if not by_slot:
        lax.fori_loop(high, bounds[2], clear, 0)

    for g in range(3):
        n = sizes[g]
        steps = lax.div(n + SIDE - 1, SIDE)

        def look(s, g=g, n=n):
            found = []
            for i in range(SIDE):
                at = g * TPD + jnp.clip(s * SIDE + i, 0, n - 1)
                t = lists[0, at]
                entries = [nbr[t * NEIGHBOURS + k] for k in range(6 + g)]
                entries = [jnp.where(e < 0, EXT, e) for e in entries]
                found.append((t, lists[1, at], *entries))
            return tuple(found)

        def step(s, carried, look=look):
            before, now = carried
            following = look(s + 1)
            mine = [sides[i] for i in range(SIDE)]
            for i in range(SIDE):
                finish(acc.at[pl.ds(5 * i, 5)], before[i][0], before[i][1], place, out)
            for i in range(SIDE):
                for q, value in enumerate(tile_sums(mine[i], now[i][2:], table, place)):
                    acc[5 * i + q] = value
            for i in range(SIDE):
                sides[i] = own_side(own_table[following[i][0]])
            return tuple(x[:2] for x in now), following

        @pl.when(n > 0)
        def _(look=look, step=step, steps=steps):
            first = look(0)
            for i in range(SIDE):
                sides[i] = own_side(own_table[first[i][0]])
            before, _ = lax.fori_loop(0, steps, step, (tuple(x[:2] for x in first), first))
            for i in range(SIDE):
                finish(acc.at[pl.ds(5 * i, 5)], before[i][0], before[i][1], place, out)


def rates_of(bounds, order, nbr, ext, count, by_slot):
    smem = pl.BlockSpec(memory_space=pltpu.SMEM)
    vmem = pl.BlockSpec(memory_space=pltpu.VMEM)
    return pl.pallas_call(
        functools.partial(rates_kernel, by_slot=by_slot),
        out_shape=jax.ShapeDtypeStruct((count, 4, 128), f32),
        in_specs=[smem] * 3 + [pl.BlockSpec(memory_space=pl.ANY)],
        out_specs=vmem,
        scratch_shapes=[
            pltpu.VMEM((EXT, 8, 128), f32),
            pltpu.VMEM((2 * STAGE, 128), f32),
            pltpu.VMEM((EXT + 8, 192, 128), bf16),
            pltpu.VMEM((2 * 64, 128), f32),
            pltpu.VMEM((TPD, 48, 128), f32),
            pltpu.VMEM((5 * SIDE, 128, 128), f32),
            pltpu.VMEM((EXT + 8, 8, 128), f32),
            pltpu.SMEM((2, 3 * TPD + SIDE), jnp.int32),
            pltpu.VMEM((8, 8, 128), f32),
            pltpu.VMEM((SIDE, 128, 96), bf16),
            pltpu.SemaphoreType.DMA,
        ],
        compiler_params=pltpu.CompilerParams(vmem_limit_bytes=56 * 2**20),
        cost_estimate=pl.CostEstimate(flops=count * 8 * 128 * 128 * 1000, bytes_accessed=4 * 2**20, transcendentals=0),
    )(bounds, order, nbr, ext)


def merge_kernel(heavy, order, mine, helped, out):
    out[...] = mine[...]

    def put(s, _):
        out[order[TPD - HELP + s]] = helped[s]
        return 0

    lax.fori_loop(0, HELP * heavy[0], put, 0)


def merge(heavy, order, mine, helped):
    smem = pl.BlockSpec(memory_space=pltpu.SMEM)
    vmem = pl.BlockSpec(memory_space=pltpu.VMEM)
    return pl.pallas_call(
        merge_kernel,
        out_shape=jax.ShapeDtypeStruct((TPD, 4, 128), f32),
        in_specs=[smem] * 2 + [vmem] * 2,
        out_specs=vmem,
    )(heavy, order, mine, helped)


def starts():
    first, at = [], TPD
    for p, q in OFFSETS:
        first.append(at)
        at += HS_CORNER if p and q else HS_FACE
    return first, at


def exchange_kernel(n_gx, n_gy, send, own, ext, outgoing, send_sem, recv_sem):
    a, b = lax.axis_index("gx"), lax.axis_index("gy")
    first, _ = starts()

    def beside(p, q):
        inside = True
        for at, step, count in ((a, p, n_gx), (b, q, n_gy)):
            if step < 0:
                inside = inside & (at > 0)
            if step > 0:
                inside = inside & (at < count - 1)
        return inside

    barrier = pltpu.get_barrier_semaphore()
    for p, q in OFFSETS:
        @pl.when(beside(p, q))
        def _(p=p, q=q):
            pl.semaphore_signal(barrier, inc=1, device_id=(a + p, b + q), device_id_type=pl.DeviceIdType.MESH)

    def pick(s, _):
        outgoing[s] = own[send[s]]
        return 0

    lax.fori_loop(0, HS_FACE, pick, 0)
    rows = 1 + jnp.where(a > 0, 1, 0) + jnp.where(a < n_gx - 1, 1, 0)
    cols = 1 + jnp.where(b > 0, 1, 0) + jnp.where(b < n_gy - 1, 1, 0)
    pl.semaphore_wait(barrier, rows * cols - 1)

    def copy(i, there):
        p, q = OFFSETS[i]
        count = HS_CORNER if p and q else HS_FACE
        return pltpu.make_async_remote_copy(
            src_ref=outgoing.at[pl.ds(0, count)],
            dst_ref=ext.at[pl.ds(first[there], count)],
            send_sem=send_sem.at[i],
            recv_sem=recv_sem.at[there],
            device_id=(a + p, b + q),
            device_id_type=pl.DeviceIdType.MESH,
        )

    for i, (p, q) in enumerate(OFFSETS):
        @pl.when(beside(p, q))
        def _(i=i, p=p, q=q):
            copy(i, OFFSETS.index((-p, -q))).start()

    def keep(b, _):
        ext[pl.ds(b * 8, 8)] = own[pl.ds(b * 8, 8)]
        return 0

    lax.fori_loop(0, TPD // 8, keep, 0)
    for i, (p, q) in enumerate(OFFSETS):
        count = HS_CORNER if p and q else HS_FACE

        @pl.when(jnp.logical_not(beside(p, q)))
        def _(i=i, count=count):
            ext[pl.ds(first[i], count)] = jnp.zeros((count, 8, 128), f32)

    for i, (p, q) in enumerate(OFFSETS):
        @pl.when(beside(p, q))
        def _(i=i, p=p, q=q):
            copy(i, OFFSETS.index((-p, -q))).wait_send()
            copy(i, i).wait_recv()


def exchange(own, send):
    vmem = pl.BlockSpec(memory_space=pltpu.VMEM)
    n_gx, n_gy = lax.axis_size("gx"), lax.axis_size("gy")

    def kernel(*refs):
        exchange_kernel(n_gx, n_gy, *refs)

    return pl.pallas_call(
        kernel,
        out_shape=jax.ShapeDtypeStruct((starts()[1], 8, 128), f32),
        in_specs=[pl.BlockSpec(memory_space=pltpu.SMEM), vmem],
        out_specs=vmem,
        scratch_shapes=[
            pltpu.VMEM((HS_FACE, 8, 128), f32),
            pltpu.SemaphoreType.DMA((8,)),
            pltpu.SemaphoreType.DMA((8,)),
        ],
        compiler_params=pltpu.CompilerParams(collective_id=0, has_side_effects=True, vmem_limit_bytes=8 * 2**20),
    )(send, own)


def shards(state, heavy_flag, order, send, nbr):
    own, order, nbr = state[0, 0], order[0, 0], nbr[0, 0].reshape(-1)
    heavy = heavy_flag[0]
    half = lax.axis_size("gx") // 2
    partners = [(g, (g + half) % (2 * half)) for g in range(2 * half)]
    ext = exchange(own, send[0, 0])
    ext_out, lists = lax.optimization_barrier((ext, jnp.concatenate([order, nbr])))
    far_ext, far_lists = (lax.ppermute(v, "gx", partners) for v in (ext_out, lists))
    live = LIGHT + (TPD - HELP - LIGHT) * heavy
    bounds = jnp.concatenate([jnp.zeros_like(live), live, jnp.where(heavy > 0, live, TPD)])
    mine = rates_of(bounds, order, nbr, ext, TPD, False)
    far_bounds = jnp.concatenate([TPD - HELP * (1 - heavy), jnp.full_like(live, TPD), jnp.full_like(live, TPD)])
    far_bounds, mine = lax.optimization_barrier((far_bounds, mine))
    helped = rates_of(far_bounds, far_lists[:TPD], far_lists[TPD:], far_ext, HELP, True)
    helped = lax.ppermute(helped, "gx", partners)
    return merge(heavy, order, mine, helped)[None, None]


def solution(mesh):
    in_specs = (
        P("gx", "gy", None, None, None),
        P("gx", "gy"),
        P("gx", "gy", None),
        P("gx", "gy", None),
        P("gx", "gy", None, None),
    )
    out_specs = P("gx", "gy", None, None, None)
    return jax.shard_map(shards, mesh=mesh, in_specs=in_specs, out_specs=out_specs, check_vma=False)
```

```python
import functools
import math

import jax
import jax.numpy as jnp
from jax import lax
from jax.experimental import pallas as pl
from jax.experimental.pallas import tpu as pltpu
from jax.sharding import PartitionSpec as P

TPD = 256
NEIGHBOURS = 8
LIGHT = 128
HS_FACE = 64
HS_CORNER = 16
EXT = 576
HELP = 48
OFFSETS = ((-1, -1), (-1, 0), (-1, 1), (0, -1), (0, 1), (1, -1), (1, 0), (1, 1))

SLOPE = -5.0 * 21.0 / (16.0 * math.pi)
ALPHA = 0.1 * math.sqrt(35.0) * 2.0
GAMMA = 2.0 / ALPHA
SOFT = 0.01 / 4.0
OWN_PART = (0, 0, 0, 1, 1, 2)
OTHER_PART = (0, 1, 2, 0, 1, 0)
BLOCKS = ((0, 0), (1, 0), (2, 0), (2, 1))
SIDE = 6
STAGE = 5 * 64
bf16, f32 = jnp.bfloat16, jnp.float32


def split3(v):
    hi = v.astype(bf16).astype(f32)
    rest = v - hi
    mid = rest.astype(bf16).astype(f32)
    return hi, mid, rest - mid


def fields(src, first):
    flat = src.reshape(src.shape[0] * 8, 128)

    def row(c):
        return flat[pl.ds(first * 8 + c, 8, stride=8), :]

    x, y, z = ((row(c) - 3.0) * 0.5 for c in range(3))
    u, v, w, rho, m = (row(c) for c in range(3, 8))
    r2 = rho * rho
    r4 = r2 * r2
    p = 5.0 * (r4 * r2 * rho - 1.0) / r2
    return x, y, z, u, v, w, rho, m, p, x * x + y * y + z * z, u * x + v * y + w * z


def other_rows(src, first):
    x, y, z, u, v, w, rho, m, p, xx, vx = fields(src, first)
    one = jnp.ones_like(x)
    gr = GAMMA * rho
    g2 = 2.0 * GAMMA
    return {
        (0, 3): 2.0 * x, (0, 4): 2.0 * y, (0, 5): 2.0 * z, (0, 7): xx,
        (1, 0): m * x, (1, 1): m * y, (1, 2): m * z, (1, 3): m * u, (1, 4): m * v, (1, 5): m * w,
        (1, 6): m, (1, 7): m * vx,
        (2, 3): 2.0 * gr * x, (2, 4): 2.0 * gr * y, (2, 5): 2.0 * gr * z, (2, 7): gr * (xx + SOFT), (2, 8): gr,
        (2, 9): g2 * x, (2, 10): g2 * y, (2, 11): g2 * z, (2, 12): GAMMA * one, (2, 13): GAMMA * xx,
        (3, 7): m * p, (3, 6): m,
    }


def own_rows(src, first):
    x, y, z, u, v, w, rho, m, p, xx, vx = fields(src, first)
    return (
        -u, -v, -w, -x, -y, -z, vx, jnp.ones_like(x),
        xx, -rho * x, -rho * y, -rho * z, rho * (xx + SOFT), rho, p,
    )


def stage_rows(src, first, stage, at):
    for (q, r), value in other_rows(src, first).items():
        b, i = (len(BLOCKS), r) if q == 3 else (BLOCKS.index((q, r // 8)), r % 8)
        stage[pl.ds(at + (b * 8 + i) * 8, 8), :] = value


def store_tables(src, first, dest, stage, at, table, place):
    zero = jnp.zeros((8, 128), f32)
    row = lax.broadcasted_iota(jnp.int32, (8, 128), 0)
    one = jnp.where(row == 0, 1.0, 0.0)
    for i in range(8):
        blocks = [split3(stage[pl.ds(at + b * 64 + i, 8, stride=8), :]) for b in range(len(BLOCKS) + 1)]
        for part in range(3):
            h, c, d, d_end, a = (block[part] for block in blocks)
            halves = (
                (h, zero if part else one),
                (c, zero),
                (d, d_end),
                (jnp.where(row == 7, a, 0.0), jnp.where(row == 6, a, 0.0)),
            )
            for q in range(4):
                to = part * 64 + q * 16
                table[dest + i, to:to + 16, :] = jnp.concatenate(halves[q], 0).astype(bf16)
        place[dest + i] = (src[first + i] - 3.0) * 0.5


def own_tables(src, first, stage, table):
    for r, value in enumerate(own_rows(src, first)):
        stage[pl.ds(r * 8, 8), :] = value
    for i in range(8):
        for h in range(2):
            for part, v in enumerate(split3(stage[pl.ds(h * 64 + i, 8, stride=8), :])):
                at = part * 16 + h * 8
                table[first + i, at:at + 8, :] = v


def own_side(rows):
    parts = [rows[i * 16:(i + 1) * 16] for i in range(3)]
    return jnp.concatenate([parts[p] for p in OWN_PART], 0).T.astype(bf16)


def other_side(table, e):
    return jnp.concatenate(
        [
            jnp.concatenate([table[e, pl.ds(p * 64 + q * 16, 16), :] for p in OTHER_PART], 0)
            for q in range(4)
        ],
        1,
    )


def pair(own, other):
    g = jnp.dot(own, other, preferred_element_type=f32)
    h, c, d, a = (g[:, i * 128:(i + 1) * 128] for i in range(4))
    h = jnp.maximum(h, 1e-30)
    reach = jnp.maximum(1.0 - h * lax.rsqrt(h), 0.0)
    cube = reach * reach * reach
    push = (a - jnp.minimum(c, 0.0) * pl.reciprocal(d, approx=True)) * cube
    return push, cube * c


def tile_sums(own, entries, table, place):
    sums = None
    for e in entries:
        push, rate = pair(own, other_side(table, e))
        new = [push * place[e, 0:1], push * place[e, 1:2], push * place[e, 2:3], push, rate]
        sums = new if sums is None else [a + b for a, b in zip(sums, new)]
    return sums


def finish(acc, t, at, place, out):
    totals = [jnp.sum(acc[q].T, 0, keepdims=True) for q in range(5)]
    out[at, 0:3] = (-2.0 * SLOPE) * (place[t][:3] * totals[3] - jnp.concatenate(totals[:3], 0))
    out[at, 3:4] = (2.0 * SLOPE) * totals[4]


def rates_kernel(bounds, order, nbr, source, out, ext, stage, table, own_stage, own_table, acc, place, lists, blank, sides, sem, *, by_slot):
    low, high = bounds[0], bounds[1]

    @pl.when(high > low)
    def _():
        fetch = pltpu.make_async_copy(source, ext, sem)
        fetch.start()
        stage[...] = jnp.zeros_like(stage)
        own_stage[...] = jnp.zeros_like(own_stage)
        blank[...] = jnp.where(lax.broadcasted_iota(jnp.int32, blank.shape, 1) == 6, 1.0, 0.0)

        fetch.wait()

        def build(b, _):
            stage_rows(ext, b * 16 + 8, stage, STAGE)
            store_tables(ext, b * 16, b * 16, stage, 0, table, place)
            stage_rows(ext, jnp.minimum(b * 16 + 16, EXT - 8), stage, 0)
            store_tables(ext, b * 16 + 8, b * 16 + 8, stage, STAGE, table, place)
            return 0

        stage_rows(ext, 0, stage, 0)
        lax.fori_loop(0, EXT // 16, build, 0)
        stage_rows(blank, 0, stage, 0)
        store_tables(blank, 0, EXT, stage, 0, table, place)

        def build_own(b, _):
            own_tables(ext, b * 8, own_stage, own_table)
            return 0

        lax.fori_loop(0, TPD // 8, build_own, 0)

    def sort(b, sizes):
        for i in range(4):
            s = low + b * 4 + i
            t = order[s]
            seven = nbr[t * NEIGHBOURS + 6] >= 0
            eight = nbr[t * NEIGHBOURS + 7] >= 0
            n = jnp.where(eight, sizes[2], jnp.where(seven, sizes[1], sizes[0]))
            at = n + jnp.where(eight, 2 * TPD, jnp.where(seven, TPD, 0))
            lists[0, at] = t
            lists[1, at] = s - low if by_slot else t
            sizes = (
                jnp.where(seven, sizes[0], sizes[0] + 1),
                jnp.where(eight, sizes[1], jnp.where(seven, sizes[1] + 1, sizes[1])),
                jnp.where(eight, sizes[2] + 1, sizes[2]),
            )
        return sizes

    none = jnp.int32(0)
    sizes = list(lax.fori_loop(0, (high - low) // 4, sort, (none, none, none)))

    for g in range(2):
        odd = lax.rem(sizes[g], SIDE)
        for i in range(SIDE - 1):
            @pl.when(i < odd)
            def _(g=g, i=i):
                for c in range(2):
                    lists[c, (g + 1) * TPD + sizes[g + 1] + i] = lists[c, g * TPD + sizes[g] - 1 - i]
        sizes[g] = sizes[g] - odd
        sizes[g + 1] = sizes[g + 1] + odd

    def clear(s, _):
        out[order[s]] = jnp.zeros((4, 128), f32)
        return 0

    if not by_slot:
        lax.fori_loop(high, bounds[2], clear, 0)

    for g in range(3):
        n = sizes[g]
        steps = lax.div(n + SIDE - 1, SIDE)

        def look(s, g=g, n=n):
            found = []
            for i in range(SIDE):
                at = g * TPD + jnp.clip(s * SIDE + i, 0, n - 1)
                t = lists[0, at]
                entries = [nbr[t * NEIGHBOURS + k] for k in range(6 + g)]
                entries = [jnp.where(e < 0, EXT, e) for e in entries]
                found.append((t, lists[1, at], *entries))
            return tuple(found)

        def step(s, carried, look=look):
            before, now = carried
            following = look(s + 1)
            mine = [sides[i] for i in range(SIDE)]
            for i in range(SIDE):
                finish(acc.at[pl.ds(5 * i, 5)], before[i][0], before[i][1], place, out)
            for i in range(SIDE):
                for q, value in enumerate(tile_sums(mine[i], now[i][2:], table, place)):
                    acc[5 * i + q] = value
            for i in range(SIDE):
                sides[i] = own_side(own_table[following[i][0]])
            return tuple(x[:2] for x in now), following

        @pl.when(n > 0)
        def _(look=look, step=step, steps=steps):
            first = look(0)
            for i in range(SIDE):
                sides[i] = own_side(own_table[first[i][0]])
            before, _ = lax.fori_loop(0, steps, step, (tuple(x[:2] for x in first), first))
            for i in range(SIDE):
                finish(acc.at[pl.ds(5 * i, 5)], before[i][0], before[i][1], place, out)


def rates_of(bounds, order, nbr, ext, count, by_slot):
    smem = pl.BlockSpec(memory_space=pltpu.SMEM)
    vmem = pl.BlockSpec(memory_space=pltpu.VMEM)
    return pl.pallas_call(
        functools.partial(rates_kernel, by_slot=by_slot),
        out_shape=jax.ShapeDtypeStruct((count, 4, 128), f32),
        in_specs=[smem] * 3 + [pl.BlockSpec(memory_space=pl.ANY)],
        out_specs=vmem,
        scratch_shapes=[
            pltpu.VMEM((EXT, 8, 128), f32),
            pltpu.VMEM((2 * STAGE, 128), f32),
            pltpu.VMEM((EXT + 8, 192, 128), bf16),
            pltpu.VMEM((2 * 64, 128), f32),
            pltpu.VMEM((TPD, 48, 128), f32),
            pltpu.VMEM((5 * SIDE, 128, 128), f32),
            pltpu.VMEM((EXT + 8, 8, 128), f32),
            pltpu.SMEM((2, 3 * TPD + SIDE), jnp.int32),
            pltpu.VMEM((8, 8, 128), f32),
            pltpu.VMEM((SIDE, 128, 96), bf16),
            pltpu.SemaphoreType.DMA,
        ],
        compiler_params=pltpu.CompilerParams(vmem_limit_bytes=62 * 2**20),
        cost_estimate=pl.CostEstimate(flops=count * 8 * 128 * 128 * 1000, bytes_accessed=4 * 2**20, transcendentals=0),
    )(bounds, order, nbr, ext)


def merge_kernel(heavy, order, mine, helped, out):
    out[...] = mine[...]

    def put(s, _):
        out[order[TPD - HELP + s]] = helped[s]
        return 0

    lax.fori_loop(0, HELP * heavy[0], put, 0)


def merge(heavy, order, mine, helped):
    smem = pl.BlockSpec(memory_space=pltpu.SMEM)
    vmem = pl.BlockSpec(memory_space=pltpu.VMEM)
    return pl.pallas_call(
        merge_kernel,
        out_shape=jax.ShapeDtypeStruct((TPD, 4, 128), f32),
        in_specs=[smem] * 2 + [vmem] * 2,
        out_specs=vmem,
    )(heavy, order, mine, helped)


def starts():
    first, at = [], TPD
    for p, q in OFFSETS:
        first.append(at)
        at += HS_CORNER if p and q else HS_FACE
    return first, at


def exchange_kernel(n_gx, n_gy, send, own, ext, outgoing, send_sem, recv_sem):
    a, b = lax.axis_index("gx"), lax.axis_index("gy")
    first, _ = starts()

    def beside(p, q):
        inside = True
        for at, step, count in ((a, p, n_gx), (b, q, n_gy)):
            if step < 0:
                inside = inside & (at > 0)
            if step > 0:
                inside = inside & (at < count - 1)
        return inside

    barrier = pltpu.get_barrier_semaphore()
    for p, q in OFFSETS:
        @pl.when(beside(p, q))
        def _(p=p, q=q):
            pl.semaphore_signal(barrier, inc=1, device_id=(a + p, b + q), device_id_type=pl.DeviceIdType.MESH)

    def pick(s, _):
        outgoing[s] = own[send[s]]
        return 0

    lax.fori_loop(0, HS_FACE, pick, 0)
    rows = 1 + jnp.where(a > 0, 1, 0) + jnp.where(a < n_gx - 1, 1, 0)
    cols = 1 + jnp.where(b > 0, 1, 0) + jnp.where(b < n_gy - 1, 1, 0)
    pl.semaphore_wait(barrier, rows * cols - 1)

    def copy(i, there):
        p, q = OFFSETS[i]
        count = HS_CORNER if p and q else HS_FACE
        return pltpu.make_async_remote_copy(
            src_ref=outgoing.at[pl.ds(0, count)],
            dst_ref=ext.at[pl.ds(first[there], count)],
            send_sem=send_sem.at[i],
            recv_sem=recv_sem.at[there],
            device_id=(a + p, b + q),
            device_id_type=pl.DeviceIdType.MESH,
        )

    for i, (p, q) in enumerate(OFFSETS):
        @pl.when(beside(p, q))
        def _(i=i, p=p, q=q):
            copy(i, OFFSETS.index((-p, -q))).start()

    def keep(b, _):
        ext[pl.ds(b * 8, 8)] = own[pl.ds(b * 8, 8)]
        return 0

    lax.fori_loop(0, TPD // 8, keep, 0)
    for i, (p, q) in enumerate(OFFSETS):
        count = HS_CORNER if p and q else HS_FACE

        @pl.when(jnp.logical_not(beside(p, q)))
        def _(i=i, count=count):
            ext[pl.ds(first[i], count)] = jnp.zeros((count, 8, 128), f32)

    for i, (p, q) in enumerate(OFFSETS):
        @pl.when(beside(p, q))
        def _(i=i, p=p, q=q):
            copy(i, OFFSETS.index((-p, -q))).wait_send()
            copy(i, i).wait_recv()


def exchange(own, send):
    vmem = pl.BlockSpec(memory_space=pltpu.VMEM)
    n_gx, n_gy = lax.axis_size("gx"), lax.axis_size("gy")

    def kernel(*refs):
        exchange_kernel(n_gx, n_gy, *refs)

    return pl.pallas_call(
        kernel,
        out_shape=jax.ShapeDtypeStruct((starts()[1], 8, 128), f32),
        in_specs=[pl.BlockSpec(memory_space=pltpu.SMEM), vmem],
        out_specs=vmem,
        scratch_shapes=[
            pltpu.VMEM((HS_FACE, 8, 128), f32),
            pltpu.SemaphoreType.DMA((8,)),
            pltpu.SemaphoreType.DMA((8,)),
        ],
        compiler_params=pltpu.CompilerParams(collective_id=0, has_side_effects=True, vmem_limit_bytes=8 * 2**20),
    )(send, own)


def swap_kernel(half, mine, theirs, send_sem, recv_sem):
    a, b = lax.axis_index("gx"), lax.axis_index("gy")
    partner = (lax.rem(a + half, 2 * half), b)
    barrier = pltpu.get_barrier_semaphore()
    pl.semaphore_signal(barrier, inc=1, device_id=partner, device_id_type=pl.DeviceIdType.MESH)
    pl.semaphore_wait(barrier, 1)
    copy = pltpu.make_async_remote_copy(
        src_ref=mine,
        dst_ref=theirs,
        send_sem=send_sem,
        recv_sem=recv_sem,
        device_id=partner,
        device_id_type=pl.DeviceIdType.MESH,
    )
    copy.start()
    copy.wait()


def swap(mine, half):
    vmem = pl.BlockSpec(memory_space=pltpu.VMEM)
    return pl.pallas_call(
        functools.partial(swap_kernel, half),
        out_shape=jax.ShapeDtypeStruct(mine.shape, mine.dtype),
        in_specs=[vmem],
        out_specs=vmem,
        scratch_shapes=[pltpu.SemaphoreType.DMA, pltpu.SemaphoreType.DMA],
        compiler_params=pltpu.CompilerParams(collective_id=1, has_side_effects=True),
    )(mine)


def shards(state, heavy_flag, order, send, nbr):
    own, order, nbr = state[0, 0], order[0, 0], nbr[0, 0].reshape(-1)
    heavy = heavy_flag[0]
    half = lax.axis_size("gx") // 2
    partners = [(g, (g + half) % (2 * half)) for g in range(2 * half)]
    ext = exchange(own, send[0, 0])
    ext_out, lists = lax.optimization_barrier((ext, jnp.concatenate([order, nbr])))
    far_ext, far_lists = (lax.ppermute(v, "gx", partners) for v in (ext_out, lists))
    live = LIGHT + (TPD - HELP - LIGHT) * heavy
    bounds = jnp.concatenate([jnp.zeros_like(live), live, jnp.where(heavy > 0, live, TPD)])
    mine = rates_of(bounds, order, nbr, ext, TPD, False)
    far_bounds = jnp.concatenate([TPD - HELP * (1 - heavy), jnp.full_like(live, TPD), jnp.full_like(live, TPD)])
    far_bounds, mine = lax.optimization_barrier((far_bounds, mine))
    helped = rates_of(far_bounds, far_lists[:TPD], far_lists[TPD:], far_ext, HELP, True)
    helped = swap(helped, half)
    return merge(heavy, order, mine, helped)[None, None]


def solution(mesh):
    in_specs = (
        P("gx", "gy", None, None, None),
        P("gx", "gy"),
        P("gx", "gy", None),
        P("gx", "gy", None),
        P("gx", "gy", None, None),
    )
    out_specs = P("gx", "gy", None, None, None)
    return jax.shard_map(shards, mesh=mesh, in_specs=in_specs, out_specs=out_specs, check_vma=False)
```

```python
import functools
import math

import jax
import jax.numpy as jnp
from jax import lax
from jax.experimental import pallas as pl
from jax.experimental.pallas import tpu as pltpu
from jax.sharding import PartitionSpec as P

TPD = 256
NEIGHBOURS = 8
LIGHT = 128
HS_FACE = 64
HS_CORNER = 16
EXT = 576
HELP = 48
OFFSETS = ((-1, -1), (-1, 0), (-1, 1), (0, -1), (0, 1), (1, -1), (1, 0), (1, 1))

SLOPE = -5.0 * 21.0 / (16.0 * math.pi)
ALPHA = 0.1 * math.sqrt(35.0) * 2.0
GAMMA = 2.0 / ALPHA
SOFT = 0.01 / 4.0
OWN_PART = (0, 0, 0, 1, 1, 2)
OTHER_PART = (0, 1, 2, 0, 1, 0)
BLOCKS = ((0, 0), (1, 0), (2, 0), (2, 1))
SIDE = 4
STAGE = 5 * 64
bf16, f32 = jnp.bfloat16, jnp.float32


def split3(v):
    hi = v.astype(bf16).astype(f32)
    rest = v - hi
    mid = rest.astype(bf16).astype(f32)
    return hi, mid, rest - mid


def fields(src, first):
    flat = src.reshape(src.shape[0] * 8, 128)

    def row(c):
        return flat[pl.ds(first * 8 + c, 8, stride=8), :]

    x, y, z = ((row(c) - 3.0) * 0.5 for c in range(3))
    u, v, w, rho, m = (row(c) for c in range(3, 8))
    r2 = rho * rho
    r4 = r2 * r2
    p = 5.0 * (r4 * r2 * rho - 1.0) / r2
    return x, y, z, u, v, w, rho, m, p, x * x + y * y + z * z, u * x + v * y + w * z


def other_rows(src, first):
    x, y, z, u, v, w, rho, m, p, xx, vx = fields(src, first)
    one = jnp.ones_like(x)
    gr = GAMMA * rho
    g2 = 2.0 * GAMMA
    return {
        (0, 3): 2.0 * x, (0, 4): 2.0 * y, (0, 5): 2.0 * z, (0, 7): xx,
        (1, 0): m * x, (1, 1): m * y, (1, 2): m * z, (1, 3): m * u, (1, 4): m * v, (1, 5): m * w,
        (1, 6): m, (1, 7): m * vx,
        (2, 3): 2.0 * gr * x, (2, 4): 2.0 * gr * y, (2, 5): 2.0 * gr * z, (2, 7): gr * (xx + SOFT), (2, 8): gr,
        (2, 9): g2 * x, (2, 10): g2 * y, (2, 11): g2 * z, (2, 12): GAMMA * one, (2, 13): GAMMA * xx,
        (3, 7): m * p, (3, 6): m,
    }


def own_rows(src, first):
    x, y, z, u, v, w, rho, m, p, xx, vx = fields(src, first)
    return (
        -u, -v, -w, -x, -y, -z, vx, jnp.ones_like(x),
        xx, -rho * x, -rho * y, -rho * z, rho * (xx + SOFT), rho, p,
    )


def stage_rows(src, first, stage, at):
    for (q, r), value in other_rows(src, first).items():
        b, i = (len(BLOCKS), r) if q == 3 else (BLOCKS.index((q, r // 8)), r % 8)
        stage[pl.ds(at + (b * 8 + i) * 8, 8), :] = value


def store_tables(src, first, dest, stage, at, table, place):
    zero = jnp.zeros((8, 128), f32)
    row = lax.broadcasted_iota(jnp.int32, (8, 128), 0)
    one = jnp.where(row == 0, 1.0, 0.0)
    for i in range(8):
        blocks = [split3(stage[pl.ds(at + b * 64 + i, 8, stride=8), :]) for b in range(len(BLOCKS) + 1)]
        for part in range(3):
            h, c, d, d_end, a = (block[part] for block in blocks)
            halves = (
                (h, zero if part else one),
                (c, zero),
                (d, d_end),
                (jnp.where(row == 7, a, 0.0), jnp.where(row == 6, a, 0.0)),
            )
            for q in range(4):
                to = part * 64 + q * 16
                table[dest + i, to:to + 16, :] = jnp.concatenate(halves[q], 0).astype(bf16)
        place[dest + i] = (src[first + i] - 3.0) * 0.5


def own_tables(src, first, stage, table):
    for r, value in enumerate(own_rows(src, first)):
        stage[pl.ds(r * 8, 8), :] = value
    for i in range(8):
        for h in range(2):
            for part, v in enumerate(split3(stage[pl.ds(h * 64 + i, 8, stride=8), :])):
                at = part * 16 + h * 8
                table[first + i, at:at + 8, :] = v


def own_side(rows):
    parts = [rows[i * 16:(i + 1) * 16] for i in range(3)]
    return jnp.concatenate([parts[p] for p in OWN_PART], 0).T.astype(bf16)


def other_side(table, e):
    return jnp.concatenate(
        [
            jnp.concatenate([table[e, pl.ds(p * 64 + q * 16, 16), :] for p in OTHER_PART], 0)
            for q in range(4)
        ],
        1,
    )


def pair(own, other):
    g = jnp.dot(own, other, preferred_element_type=f32)
    h, c, d, a = (g[:, i * 128:(i + 1) * 128] for i in range(4))
    h = jnp.maximum(h, 1e-30)
    reach = jnp.maximum(1.0 - h * lax.rsqrt(h), 0.0)
    cube = reach * reach * reach
    push = (a - jnp.minimum(c, 0.0) * pl.reciprocal(d, approx=True)) * cube
    return push, cube * c


def tile_sums(own, entries, table, place):
    sums = None
    for e in entries:
        push, rate = pair(own, other_side(table, e))
        new = [push * place[e, 0:1], push * place[e, 1:2], push * place[e, 2:3], push, rate]
        sums = new if sums is None else [a + b for a, b in zip(sums, new)]
    return sums


def finish(acc, t, at, place, out):
    totals = [jnp.sum(acc[q].T, 0, keepdims=True) for q in range(5)]
    out[at, 0:3] = (-2.0 * SLOPE) * (place[t][:3] * totals[3] - jnp.concatenate(totals[:3], 0))
    out[at, 3:4] = (2.0 * SLOPE) * totals[4]


def rates_kernel(bounds, order, nbr, source, out, ext, stage, table, own_stage, own_table, acc, place, lists, blank, sides, sem, *, by_slot):
    low, high = bounds[0], bounds[1]

    @pl.when(high > low)
    def _():
        fetch = pltpu.make_async_copy(source, ext, sem)
        fetch.start()
        stage[...] = jnp.zeros_like(stage)
        own_stage[...] = jnp.zeros_like(own_stage)
        blank[...] = jnp.where(lax.broadcasted_iota(jnp.int32, blank.shape, 1) == 6, 1.0, 0.0)

        fetch.wait()

        def build(b, _):
            stage_rows(ext, b * 16 + 8, stage, STAGE)
            store_tables(ext, b * 16, b * 16, stage, 0, table, place)
            stage_rows(ext, jnp.minimum(b * 16 + 16, EXT - 8), stage, 0)
            store_tables(ext, b * 16 + 8, b * 16 + 8, stage, STAGE, table, place)
            return 0

        stage_rows(ext, 0, stage, 0)
        lax.fori_loop(0, EXT // 16, build, 0)
        stage_rows(blank, 0, stage, 0)
        store_tables(blank, 0, EXT, stage, 0, table, place)

        def build_own(b, _):
            own_tables(ext, b * 8, own_stage, own_table)
            return 0

        lax.fori_loop(0, TPD // 8, build_own, 0)

    def sort(b, sizes):
        for i in range(4):
            s = low + b * 4 + i
            t = order[s]
            seven = nbr[t * NEIGHBOURS + 6] >= 0
            eight = nbr[t * NEIGHBOURS + 7] >= 0
            n = jnp.where(eight, sizes[2], jnp.where(seven, sizes[1], sizes[0]))
            at = n + jnp.where(eight, 2 * TPD, jnp.where(seven, TPD, 0))
            lists[0, at] = t
            lists[1, at] = s - low if by_slot else t
            sizes = (
                jnp.where(seven, sizes[0], sizes[0] + 1),
                jnp.where(eight, sizes[1], jnp.where(seven, sizes[1] + 1, sizes[1])),
                jnp.where(eight, sizes[2] + 1, sizes[2]),
            )
        return sizes

    none = jnp.int32(0)
    sizes = list(lax.fori_loop(0, (high - low) // 4, sort, (none, none, none)))

    for g in range(2):
        odd = lax.rem(sizes[g], SIDE)
        for i in range(SIDE - 1):
            @pl.when(i < odd)
            def _(g=g, i=i):
                for c in range(2):
                    lists[c, (g + 1) * TPD + sizes[g + 1] + i] = lists[c, g * TPD + sizes[g] - 1 - i]
        sizes[g] = sizes[g] - odd
        sizes[g + 1] = sizes[g + 1] + odd

    def clear(s, _):
        out[order[s]] = jnp.zeros((4, 128), f32)
        return 0

    if not by_slot:
        lax.fori_loop(high, bounds[2], clear, 0)

    for g in range(3):
        n = sizes[g]
        steps = lax.div(n + SIDE - 1, SIDE)

        def look(s, g=g, n=n):
            found = []
            for i in range(SIDE):
                at = g * TPD + jnp.clip(s * SIDE + i, 0, n - 1)
                t = lists[0, at]
                entries = [nbr[t * NEIGHBOURS + k] for k in range(6 + g)]
                entries = [jnp.where(e < 0, EXT, e) for e in entries]
                found.append((t, lists[1, at], *entries))
            return tuple(found)

        def step(s, carried, look=look):
            before, now = carried
            following = look(s + 1)
            mine = [sides[i] for i in range(SIDE)]
            for i in range(SIDE):
                finish(acc.at[pl.ds(5 * i, 5)], before[i][0], before[i][1], place, out)
            for i in range(SIDE):
                for q, value in enumerate(tile_sums(mine[i], now[i][2:], table, place)):
                    acc[5 * i + q] = value
            for i in range(SIDE):
                sides[i] = own_side(own_table[following[i][0]])
            return tuple(x[:2] for x in now), following

        @pl.when(n > 0)
        def _(look=look, step=step, steps=steps):
            first = look(0)
            for i in range(SIDE):
                sides[i] = own_side(own_table[first[i][0]])
            before, _ = lax.fori_loop(0, steps, step, (tuple(x[:2] for x in first), first))
            for i in range(SIDE):
                finish(acc.at[pl.ds(5 * i, 5)], before[i][0], before[i][1], place, out)


def rates_of(bounds, order, nbr, ext, count, by_slot):
    smem = pl.BlockSpec(memory_space=pltpu.SMEM)
    vmem = pl.BlockSpec(memory_space=pltpu.VMEM)
    return pl.pallas_call(
        functools.partial(rates_kernel, by_slot=by_slot),
        out_shape=jax.ShapeDtypeStruct((count, 4, 128), f32),
        in_specs=[smem] * 3 + [pl.BlockSpec(memory_space=pl.ANY)],
        out_specs=vmem,
        scratch_shapes=[
            pltpu.VMEM((EXT, 8, 128), f32),
            pltpu.VMEM((2 * STAGE, 128), f32),
            pltpu.VMEM((EXT + 8, 192, 128), bf16),
            pltpu.VMEM((2 * 64, 128), f32),
            pltpu.VMEM((TPD, 48, 128), f32),
            pltpu.VMEM((5 * SIDE, 128, 128), f32),
            pltpu.VMEM((EXT + 8, 8, 128), f32),
            pltpu.SMEM((2, 3 * TPD + SIDE), jnp.int32),
            pltpu.VMEM((8, 8, 128), f32),
            pltpu.VMEM((SIDE, 128, 96), bf16),
            pltpu.SemaphoreType.DMA,
        ],
        compiler_params=pltpu.CompilerParams(vmem_limit_bytes=62 * 2**20),
        cost_estimate=pl.CostEstimate(flops=count * 8 * 128 * 128 * 1000, bytes_accessed=4 * 2**20, transcendentals=0),
    )(bounds, order, nbr, ext)


def merge_kernel(heavy, order, mine, helped, out):
    out[...] = mine[...]

    def put(s, _):
        out[order[TPD - HELP + s]] = helped[s]
        return 0

    lax.fori_loop(0, HELP * heavy[0], put, 0)


def merge(heavy, order, mine, helped):
    smem = pl.BlockSpec(memory_space=pltpu.SMEM)
    vmem = pl.BlockSpec(memory_space=pltpu.VMEM)
    return pl.pallas_call(
        merge_kernel,
        out_shape=jax.ShapeDtypeStruct((TPD, 4, 128), f32),
        in_specs=[smem] * 2 + [vmem] * 2,
        out_specs=vmem,
    )(heavy, order, mine, helped)


def starts():
    first, at = [], TPD
    for p, q in OFFSETS:
        first.append(at)
        at += HS_CORNER if p and q else HS_FACE
    return first, at


def exchange_kernel(n_gx, n_gy, send, source, ext, own, outgoing, fetch_sem, send_sem, recv_sem):
    a, b = lax.axis_index("gx"), lax.axis_index("gy")
    first, _ = starts()

    def beside(p, q):
        inside = True
        for at, step, count in ((a, p, n_gx), (b, q, n_gy)):
            if step < 0:
                inside = inside & (at > 0)
            if step > 0:
                inside = inside & (at < count - 1)
        return inside

    fetch = pltpu.make_async_copy(source, own, fetch_sem)
    fetch.start()
    barrier = pltpu.get_barrier_semaphore()
    for p, q in OFFSETS:
        @pl.when(beside(p, q))
        def _(p=p, q=q):
            pl.semaphore_signal(barrier, inc=1, device_id=(a + p, b + q), device_id_type=pl.DeviceIdType.MESH)

    def pick(s, _):
        outgoing[s] = own[send[s]]
        return 0

    fetch.wait()
    lax.fori_loop(0, HS_FACE, pick, 0)
    rows = 1 + jnp.where(a > 0, 1, 0) + jnp.where(a < n_gx - 1, 1, 0)
    cols = 1 + jnp.where(b > 0, 1, 0) + jnp.where(b < n_gy - 1, 1, 0)
    pl.semaphore_wait(barrier, rows * cols - 1)

    def copy(i, there):
        p, q = OFFSETS[i]
        count = HS_CORNER if p and q else HS_FACE
        return pltpu.make_async_remote_copy(
            src_ref=outgoing.at[pl.ds(0, count)],
            dst_ref=ext.at[pl.ds(first[there], count)],
            send_sem=send_sem.at[i],
            recv_sem=recv_sem.at[there],
            device_id=(a + p, b + q),
            device_id_type=pl.DeviceIdType.MESH,
        )

    for i, (p, q) in enumerate(OFFSETS):
        @pl.when(beside(p, q))
        def _(i=i, p=p, q=q):
            copy(i, OFFSETS.index((-p, -q))).start()

    def keep(b, _):
        ext[pl.ds(b * 8, 8)] = own[pl.ds(b * 8, 8)]
        return 0

    lax.fori_loop(0, TPD // 8, keep, 0)
    for i, (p, q) in enumerate(OFFSETS):
        count = HS_CORNER if p and q else HS_FACE

        @pl.when(jnp.logical_not(beside(p, q)))
        def _(i=i, count=count):
            ext[pl.ds(first[i], count)] = jnp.zeros((count, 8, 128), f32)

    for i, (p, q) in enumerate(OFFSETS):
        @pl.when(beside(p, q))
        def _(i=i, p=p, q=q):
            copy(i, OFFSETS.index((-p, -q))).wait_send()
            copy(i, i).wait_recv()


def exchange(own, send):
    vmem = pl.BlockSpec(memory_space=pltpu.VMEM)
    n_gx, n_gy = lax.axis_size("gx"), lax.axis_size("gy")

    def kernel(*refs):
        exchange_kernel(n_gx, n_gy, *refs)

    return pl.pallas_call(
        kernel,
        out_shape=jax.ShapeDtypeStruct((starts()[1], 8, 128), f32),
        in_specs=[pl.BlockSpec(memory_space=pltpu.SMEM), pl.BlockSpec(memory_space=pl.ANY)],
        out_specs=vmem,
        scratch_shapes=[
            pltpu.VMEM((TPD, 8, 128), f32),
            pltpu.VMEM((HS_FACE, 8, 128), f32),
            pltpu.SemaphoreType.DMA,
            pltpu.SemaphoreType.DMA((8,)),
            pltpu.SemaphoreType.DMA((8,)),
        ],
        compiler_params=pltpu.CompilerParams(collective_id=0, has_side_effects=True, vmem_limit_bytes=62 * 2**20),
    )(send, own)


def swap_kernel(half, mine, theirs, send_sem, recv_sem):
    a, b = lax.axis_index("gx"), lax.axis_index("gy")
    partner = (lax.rem(a + half, 2 * half), b)
    barrier = pltpu.get_barrier_semaphore()
    pl.semaphore_signal(barrier, inc=1, device_id=partner, device_id_type=pl.DeviceIdType.MESH)
    pl.semaphore_wait(barrier, 1)
    copy = pltpu.make_async_remote_copy(
        src_ref=mine,
        dst_ref=theirs,
        send_sem=send_sem,
        recv_sem=recv_sem,
        device_id=partner,
        device_id_type=pl.DeviceIdType.MESH,
    )
    copy.start()
    copy.wait()


def swap(mine, half):
    vmem = pl.BlockSpec(memory_space=pltpu.VMEM)
    return pl.pallas_call(
        functools.partial(swap_kernel, half),
        out_shape=jax.ShapeDtypeStruct(mine.shape, mine.dtype),
        in_specs=[vmem],
        out_specs=vmem,
        scratch_shapes=[pltpu.SemaphoreType.DMA, pltpu.SemaphoreType.DMA],
        compiler_params=pltpu.CompilerParams(collective_id=1, has_side_effects=True),
    )(mine)


def shards(state, heavy_flag, order, send, nbr):
    own, order, nbr = state[0, 0], order[0, 0], nbr[0, 0].reshape(-1)
    heavy = heavy_flag[0]
    half = lax.axis_size("gx") // 2
    partners = [(g, (g + half) % (2 * half)) for g in range(2 * half)]
    ext = exchange(own, send[0, 0])
    ext_out, lists = lax.optimization_barrier((ext, jnp.concatenate([order, nbr])))
    far_ext, far_lists = (lax.ppermute(v, "gx", partners) for v in (ext_out, lists))
    live = LIGHT + (TPD - HELP - LIGHT) * heavy
    bounds = jnp.concatenate([jnp.zeros_like(live), live, jnp.where(heavy > 0, live, TPD)])
    mine = rates_of(bounds, order, nbr, ext, TPD, False)
    far_bounds = jnp.concatenate([TPD - HELP * (1 - heavy), jnp.full_like(live, TPD), jnp.full_like(live, TPD)])
    far_bounds, mine = lax.optimization_barrier((far_bounds, mine))
    helped = rates_of(far_bounds, far_lists[:TPD], far_lists[TPD:], far_ext, HELP, True)
    helped = swap(helped, half)
    return merge(heavy, order, mine, helped)[None, None]


def solution(mesh):
    in_specs = (
        P("gx", "gy", None, None, None),
        P("gx", "gy"),
        P("gx", "gy", None),
        P("gx", "gy", None),
        P("gx", "gy", None, None),
    )
    out_specs = P("gx", "gy", None, None, None)
    return jax.shard_map(shards, mesh=mesh, in_specs=in_specs, out_specs=out_specs, check_vma=False)
```

```python
import functools
import math

import jax
import jax.numpy as jnp
from jax import lax
from jax.experimental import pallas as pl
from jax.experimental.pallas import tpu as pltpu
from jax.sharding import PartitionSpec as P

TPD = 256
NEIGHBOURS = 8
LIGHT = 128
HS_FACE = 64
HS_CORNER = 16
EXT = 576
HELP = 52
OFFSETS = ((-1, -1), (-1, 0), (-1, 1), (0, -1), (0, 1), (1, -1), (1, 0), (1, 1))

SLOPE = -5.0 * 21.0 / (16.0 * math.pi)
ALPHA = 0.1 * math.sqrt(35.0) * 2.0
GAMMA = 2.0 / ALPHA
SOFT = 0.01 / 4.0
OWN_PART = (0, 0, 0, 1, 1, 2)
OTHER_PART = (0, 1, 2, 0, 1, 0)
BLOCKS = ((0, 0), (1, 0), (2, 0), (2, 1))
SIDE = 4
STAGE = 5 * 64
bf16, f32 = jnp.bfloat16, jnp.float32


def split3(v):
    hi = v.astype(bf16).astype(f32)
    rest = v - hi
    mid = rest.astype(bf16).astype(f32)
    return hi, mid, rest - mid


def fields(src, first):
    flat = src.reshape(src.shape[0] * 8, 128)

    def row(c):
        return flat[pl.ds(first * 8 + c, 8, stride=8), :]

    x, y, z = ((row(c) - 3.0) * 0.5 for c in range(3))
    u, v, w, rho, m = (row(c) for c in range(3, 8))
    r2 = rho * rho
    r4 = r2 * r2
    p = 5.0 * (r4 * r2 * rho - 1.0) / r2
    return x, y, z, u, v, w, rho, m, p, x * x + y * y + z * z, u * x + v * y + w * z


def other_rows(src, first):
    x, y, z, u, v, w, rho, m, p, xx, vx = fields(src, first)
    one = jnp.ones_like(x)
    gr = GAMMA * rho
    g2 = 2.0 * GAMMA
    return {
        (0, 3): 2.0 * x, (0, 4): 2.0 * y, (0, 5): 2.0 * z, (0, 7): xx,
        (1, 0): m * x, (1, 1): m * y, (1, 2): m * z, (1, 3): m * u, (1, 4): m * v, (1, 5): m * w,
        (1, 6): m, (1, 7): m * vx,
        (2, 3): 2.0 * gr * x, (2, 4): 2.0 * gr * y, (2, 5): 2.0 * gr * z, (2, 7): gr * (xx + SOFT), (2, 8): gr,
        (2, 9): g2 * x, (2, 10): g2 * y, (2, 11): g2 * z, (2, 12): GAMMA * one, (2, 13): GAMMA * xx,
        (3, 7): m * p, (3, 6): m,
    }


def own_rows(src, first):
    x, y, z, u, v, w, rho, m, p, xx, vx = fields(src, first)
    return (
        -u, -v, -w, -x, -y, -z, vx, jnp.ones_like(x),
        xx, -rho * x, -rho * y, -rho * z, rho * (xx + SOFT), rho, p,
    )


def stage_rows(src, first, stage, at):
    for (q, r), value in other_rows(src, first).items():
        b, i = (len(BLOCKS), r) if q == 3 else (BLOCKS.index((q, r // 8)), r % 8)
        stage[pl.ds(at + (b * 8 + i) * 8, 8), :] = value


def store_tables(src, first, dest, stage, at, table, place):
    zero = jnp.zeros((8, 128), f32)
    row = lax.broadcasted_iota(jnp.int32, (8, 128), 0)
    one = jnp.where(row == 0, 1.0, 0.0)
    for i in range(8):
        blocks = [split3(stage[pl.ds(at + b * 64 + i, 8, stride=8), :]) for b in range(len(BLOCKS) + 1)]
        for part in range(3):
            h, c, d, d_end, a = (block[part] for block in blocks)
            halves = (
                (h, zero if part else one),
                (c, zero),
                (d, d_end),
                (jnp.where(row == 7, a, 0.0), jnp.where(row == 6, a, 0.0)),
            )
            for q in range(4):
                to = part * 64 + q * 16
                table[dest + i, to:to + 16, :] = jnp.concatenate(halves[q], 0).astype(bf16)
        place[dest + i] = (src[first + i] - 3.0) * 0.5


def own_tables(src, first, stage, table):
    for r, value in enumerate(own_rows(src, first)):
        stage[pl.ds(r * 8, 8), :] = value
    for i in range(8):
        for h in range(2):
            for part, v in enumerate(split3(stage[pl.ds(h * 64 + i, 8, stride=8), :])):
                at = part * 16 + h * 8
                table[first + i, at:at + 8, :] = v


def own_side(rows):
    parts = [rows[i * 16:(i + 1) * 16] for i in range(3)]
    return jnp.concatenate([parts[p] for p in OWN_PART], 0).T.astype(bf16)


def other_side(table, e):
    return jnp.concatenate(
        [
            jnp.concatenate([table[e, pl.ds(p * 64 + q * 16, 16), :] for p in OTHER_PART], 0)
            for q in range(4)
        ],
        1,
    )


def pair(own, other):
    g = jnp.dot(own, other, preferred_element_type=f32)
    h, c, d, a = (g[:, i * 128:(i + 1) * 128] for i in range(4))
    h = jnp.maximum(h, 1e-30)
    reach = jnp.maximum(1.0 - h * lax.rsqrt(h), 0.0)
    cube = reach * reach * reach
    push = (a - jnp.minimum(c, 0.0) * pl.reciprocal(d, approx=True)) * cube
    return push, cube * c


def tile_sums(own, entries, table, place):
    sums = None
    for e in entries:
        push, rate = pair(own, other_side(table, e))
        new = [push * place[e, 0:1], push * place[e, 1:2], push * place[e, 2:3], push, rate]
        sums = new if sums is None else [a + b for a, b in zip(sums, new)]
    return sums


def finish(acc, t, at, place, out):
    totals = [jnp.sum(acc[q].T, 0, keepdims=True) for q in range(5)]
    out[at, 0:3] = (-2.0 * SLOPE) * (place[t][:3] * totals[3] - jnp.concatenate(totals[:3], 0))
    out[at, 3:4] = (2.0 * SLOPE) * totals[4]


def rates_kernel(bounds, order, nbr, source, out, ext, stage, table, own_stage, own_table, acc, place, lists, blank, sides, sem, *, by_slot):
    low, high = bounds[0], bounds[1]

    @pl.when(high > low)
    def _():
        fetch = pltpu.make_async_copy(source, ext, sem)
        fetch.start()
        stage[...] = jnp.zeros_like(stage)
        own_stage[...] = jnp.zeros_like(own_stage)
        blank[...] = jnp.where(lax.broadcasted_iota(jnp.int32, blank.shape, 1) == 6, 1.0, 0.0)

        fetch.wait()

        def build(b, _):
            stage_rows(ext, b * 16 + 8, stage, STAGE)
            store_tables(ext, b * 16, b * 16, stage, 0, table, place)
            stage_rows(ext, jnp.minimum(b * 16 + 16, EXT - 8), stage, 0)
            store_tables(ext, b * 16 + 8, b * 16 + 8, stage, STAGE, table, place)
            return 0

        stage_rows(ext, 0, stage, 0)
        lax.fori_loop(0, EXT // 16, build, 0)
        stage_rows(blank, 0, stage, 0)
        store_tables(blank, 0, EXT, stage, 0, table, place)

        def build_own(b, _):
            own_tables(ext, b * 8, own_stage, own_table)
            return 0

        lax.fori_loop(0, TPD // 8, build_own, 0)

    def sort(b, sizes):
        for i in range(4):
            s = low + b * 4 + i
            t = order[s]
            seven = nbr[t * NEIGHBOURS + 6] >= 0
            eight = nbr[t * NEIGHBOURS + 7] >= 0
            n = jnp.where(eight, sizes[2], jnp.where(seven, sizes[1], sizes[0]))
            at = n + jnp.where(eight, 2 * TPD, jnp.where(seven, TPD, 0))
            lists[0, at] = t
            lists[1, at] = s - low if by_slot else t
            sizes = (
                jnp.where(seven, sizes[0], sizes[0] + 1),
                jnp.where(eight, sizes[1], jnp.where(seven, sizes[1] + 1, sizes[1])),
                jnp.where(eight, sizes[2] + 1, sizes[2]),
            )
        return sizes

    none = jnp.int32(0)
    sizes = list(lax.fori_loop(0, (high - low) // 4, sort, (none, none, none)))

    for g in range(2):
        odd = lax.rem(sizes[g], SIDE)
        for i in range(SIDE - 1):
            @pl.when(i < odd)
            def _(g=g, i=i):
                for c in range(2):
                    lists[c, (g + 1) * TPD + sizes[g + 1] + i] = lists[c, g * TPD + sizes[g] - 1 - i]
        sizes[g] = sizes[g] - odd
        sizes[g + 1] = sizes[g + 1] + odd

    def clear(s, _):
        out[order[s]] = jnp.zeros((4, 128), f32)
        return 0

    if not by_slot:
        lax.fori_loop(high, bounds[2], clear, 0)

    for g in range(3):
        n = sizes[g]
        steps = lax.div(n + SIDE - 1, SIDE)

        def look(s, g=g, n=n):
            found = []
            for i in range(SIDE):
                at = g * TPD + jnp.clip(s * SIDE + i, 0, n - 1)
                t = lists[0, at]
                entries = [nbr[t * NEIGHBOURS + k] for k in range(6 + g)]
                entries = [jnp.where(e < 0, EXT, e) for e in entries]
                found.append((t, lists[1, at], *entries))
            return tuple(found)

        def step(s, carried, look=look):
            before, now = carried
            following = look(s + 1)
            mine = [sides[i] for i in range(SIDE)]
            for i in range(SIDE):
                finish(acc.at[pl.ds(5 * i, 5)], before[i][0], before[i][1], place, out)
            for i in range(SIDE):
                for q, value in enumerate(tile_sums(mine[i], now[i][2:], table, place)):
                    acc[5 * i + q] = value
            for i in range(SIDE):
                sides[i] = own_side(own_table[following[i][0]])
            return tuple(x[:2] for x in now), following

        @pl.when(n > 0)
        def _(look=look, step=step, steps=steps):
            first = look(0)
            for i in range(SIDE):
                sides[i] = own_side(own_table[first[i][0]])
            before, _ = lax.fori_loop(0, steps, step, (tuple(x[:2] for x in first), first))
            for i in range(SIDE):
                finish(acc.at[pl.ds(5 * i, 5)], before[i][0], before[i][1], place, out)


def rates_of(bounds, order, nbr, ext, count, by_slot):
    smem = pl.BlockSpec(memory_space=pltpu.SMEM)
    vmem = pl.BlockSpec(memory_space=pltpu.VMEM)
    return pl.pallas_call(
        functools.partial(rates_kernel, by_slot=by_slot),
        out_shape=jax.ShapeDtypeStruct((count, 4, 128), f32),
        in_specs=[smem] * 3 + [pl.BlockSpec(memory_space=pl.ANY)],
        out_specs=vmem,
        scratch_shapes=[
            pltpu.VMEM((EXT, 8, 128), f32),
            pltpu.VMEM((2 * STAGE, 128), f32),
            pltpu.VMEM((EXT + 8, 192, 128), bf16),
            pltpu.VMEM((2 * 64, 128), f32),
            pltpu.VMEM((TPD, 48, 128), f32),
            pltpu.VMEM((5 * SIDE, 128, 128), f32),
            pltpu.VMEM((EXT + 8, 8, 128), f32),
            pltpu.SMEM((2, 3 * TPD + SIDE), jnp.int32),
            pltpu.VMEM((8, 8, 128), f32),
            pltpu.VMEM((SIDE, 128, 96), bf16),
            pltpu.SemaphoreType.DMA,
        ],
        compiler_params=pltpu.CompilerParams(vmem_limit_bytes=62 * 2**20),
        cost_estimate=pl.CostEstimate(flops=count * 8 * 128 * 128 * 1000, bytes_accessed=4 * 2**20, transcendentals=0),
    )(bounds, order, nbr, ext)


def merge_kernel(heavy, order, mine, helped, out):
    out[...] = mine[...]

    def put(s, _):
        out[order[TPD - HELP + s]] = helped[s]
        return 0

    lax.fori_loop(0, HELP * heavy[0], put, 0)


def merge(heavy, order, mine, helped):
    smem = pl.BlockSpec(memory_space=pltpu.SMEM)
    vmem = pl.BlockSpec(memory_space=pltpu.VMEM)
    return pl.pallas_call(
        merge_kernel,
        out_shape=jax.ShapeDtypeStruct((TPD, 4, 128), f32),
        in_specs=[smem] * 2 + [vmem] * 2,
        out_specs=vmem,
    )(heavy, order, mine, helped)


def starts():
    first, at = [], TPD
    for p, q in OFFSETS:
        first.append(at)
        at += HS_CORNER if p and q else HS_FACE
    return first, at


def exchange_kernel(n_gx, n_gy, send, source, ext, own, outgoing, fetch_sem, send_sem, recv_sem):
    a, b = lax.axis_index("gx"), lax.axis_index("gy")
    first, _ = starts()

    def beside(p, q):
        inside = True
        for at, step, count in ((a, p, n_gx), (b, q, n_gy)):
            if step < 0:
                inside = inside & (at > 0)
            if step > 0:
                inside = inside & (at < count - 1)
        return inside

    fetch = pltpu.make_async_copy(source, own, fetch_sem)
    fetch.start()
    barrier = pltpu.get_barrier_semaphore()
    for p, q in OFFSETS:
        @pl.when(beside(p, q))
        def _(p=p, q=q):
            pl.semaphore_signal(barrier, inc=1, device_id=(a + p, b + q), device_id_type=pl.DeviceIdType.MESH)

    def pick(s, _):
        outgoing[s] = own[send[s]]
        return 0

    fetch.wait()
    lax.fori_loop(0, HS_FACE, pick, 0)
    rows = 1 + jnp.where(a > 0, 1, 0) + jnp.where(a < n_gx - 1, 1, 0)
    cols = 1 + jnp.where(b > 0, 1, 0) + jnp.where(b < n_gy - 1, 1, 0)
    pl.semaphore_wait(barrier, rows * cols - 1)

    def copy(i, there):
        p, q = OFFSETS[i]
        count = HS_CORNER if p and q else HS_FACE
        return pltpu.make_async_remote_copy(
            src_ref=outgoing.at[pl.ds(0, count)],
            dst_ref=ext.at[pl.ds(first[there], count)],
            send_sem=send_sem.at[i],
            recv_sem=recv_sem.at[there],
            device_id=(a + p, b + q),
            device_id_type=pl.DeviceIdType.MESH,
        )

    for i, (p, q) in enumerate(OFFSETS):
        @pl.when(beside(p, q))
        def _(i=i, p=p, q=q):
            copy(i, OFFSETS.index((-p, -q))).start()

    def keep(b, _):
        ext[pl.ds(b * 8, 8)] = own[pl.ds(b * 8, 8)]
        return 0

    lax.fori_loop(0, TPD // 8, keep, 0)
    for i, (p, q) in enumerate(OFFSETS):
        count = HS_CORNER if p and q else HS_FACE

        @pl.when(jnp.logical_not(beside(p, q)))
        def _(i=i, count=count):
            ext[pl.ds(first[i], count)] = jnp.zeros((count, 8, 128), f32)

    for i, (p, q) in enumerate(OFFSETS):
        @pl.when(beside(p, q))
        def _(i=i, p=p, q=q):
            copy(i, OFFSETS.index((-p, -q))).wait_send()
            copy(i, i).wait_recv()


def exchange(own, send):
    vmem = pl.BlockSpec(memory_space=pltpu.VMEM)
    n_gx, n_gy = lax.axis_size("gx"), lax.axis_size("gy")

    def kernel(*refs):
        exchange_kernel(n_gx, n_gy, *refs)

    return pl.pallas_call(
        kernel,
        out_shape=jax.ShapeDtypeStruct((starts()[1], 8, 128), f32),
        in_specs=[pl.BlockSpec(memory_space=pltpu.SMEM), pl.BlockSpec(memory_space=pl.ANY)],
        out_specs=vmem,
        scratch_shapes=[
            pltpu.VMEM((TPD, 8, 128), f32),
            pltpu.VMEM((HS_FACE, 8, 128), f32),
            pltpu.SemaphoreType.DMA,
            pltpu.SemaphoreType.DMA((8,)),
            pltpu.SemaphoreType.DMA((8,)),
        ],
        compiler_params=pltpu.CompilerParams(collective_id=0, has_side_effects=True, vmem_limit_bytes=62 * 2**20),
    )(send, own)


def swap_kernel(half, mine, theirs, send_sem, recv_sem):
    a, b = lax.axis_index("gx"), lax.axis_index("gy")
    partner = (lax.rem(a + half, 2 * half), b)
    barrier = pltpu.get_barrier_semaphore()
    pl.semaphore_signal(barrier, inc=1, device_id=partner, device_id_type=pl.DeviceIdType.MESH)
    pl.semaphore_wait(barrier, 1)
    copy = pltpu.make_async_remote_copy(
        src_ref=mine,
        dst_ref=theirs,
        send_sem=send_sem,
        recv_sem=recv_sem,
        device_id=partner,
        device_id_type=pl.DeviceIdType.MESH,
    )
    copy.start()
    copy.wait()


def swap(mine, half):
    vmem = pl.BlockSpec(memory_space=pltpu.VMEM)
    return pl.pallas_call(
        functools.partial(swap_kernel, half),
        out_shape=jax.ShapeDtypeStruct(mine.shape, mine.dtype),
        in_specs=[vmem],
        out_specs=vmem,
        scratch_shapes=[pltpu.SemaphoreType.DMA, pltpu.SemaphoreType.DMA],
        compiler_params=pltpu.CompilerParams(collective_id=1, has_side_effects=True),
    )(mine)


def shards(state, heavy_flag, order, send, nbr):
    own, order, nbr = state[0, 0], order[0, 0], nbr[0, 0].reshape(-1)
    heavy = heavy_flag[0]
    half = lax.axis_size("gx") // 2
    partners = [(g, (g + half) % (2 * half)) for g in range(2 * half)]
    ext = exchange(own, send[0, 0])
    ext_out, lists = lax.optimization_barrier((ext, jnp.concatenate([order, nbr])))
    far_ext, far_lists = (lax.ppermute(v, "gx", partners) for v in (ext_out, lists))
    live = LIGHT + (TPD - HELP - LIGHT) * heavy
    bounds = jnp.concatenate([jnp.zeros_like(live), live, jnp.where(heavy > 0, live, TPD)])
    mine = rates_of(bounds, order, nbr, ext, TPD, False)
    far_bounds = jnp.concatenate([TPD - HELP * (1 - heavy), jnp.full_like(live, TPD), jnp.full_like(live, TPD)])
    far_bounds, mine = lax.optimization_barrier((far_bounds, mine))
    helped = rates_of(far_bounds, far_lists[:TPD], far_lists[TPD:], far_ext, HELP, True)
    helped = swap(helped, half)
    return merge(heavy, order, mine, helped)[None, None]


def solution(mesh):
    in_specs = (
        P("gx", "gy", None, None, None),
        P("gx", "gy"),
        P("gx", "gy", None),
        P("gx", "gy", None),
        P("gx", "gy", None, None),
    )
    out_specs = P("gx", "gy", None, None, None)
    return jax.shard_map(shards, mesh=mesh, in_specs=in_specs, out_specs=out_specs, check_vma=False)
```
